32 devices in a mesh: gx: 4 (over y, x), gy: 8 (over z, core).
Axes of the slice: x: 2, y: 2, z: 4, core: 2. Of those that a mesh axis runs over, the one named last changes fastest.
Arguments:
- inputs: bfloat16 [32, 32, 8, 128], P('gx', 'gy'), may hold values from -6 to 6
- preact: bfloat16 [32, 32, 8, 128], P('gx', 'gy'), may hold values from -6 to 6
- cotangent: bfloat16 [32, 32, 8, 128], P('gx', 'gy'), may hold values from -6 to 6
- spectral_w: bfloat16 [32, 32, 8, 128, 128], P('gx', 'gy'), may hold values from -2 to 2
- skip_w: bfloat16 [128, 128], replicated, may hold values from -0.5 to 0.5
Outputs:
- grad_inputs: bfloat16 [32, 32, 8, 128], P('gx', 'gy')
- grad_spectral: bfloat16 [32, 32, 8, 128, 128], P('gx', 'gy')
- grad_skip: float32 [128, 128], replicated
The draws below stay inside these ranges and needn't reach their ends.
All inputs are finite; a program needn't handle non-finite values.
Results may differ from the reference program's by a relative error of at most 0.0054.
Values may be sent and summed in bfloat16 or wider, within the bound.
No kernel may reach another device: no remote copies, remote signals or barrier semaphores. Data moves between devices by JAX's collectives and lax.ppermute only.
A program may use at most 64 MiB of HBM per device.

```python
import math
import jax
import jax.numpy as jnp
from jax import lax

C = 128
MX = 32
MY = 32
MZ = 8
NZ = 8
NX = 32
NY = 32


def shard_levels(key, extent, pieces, smallest, largest):
    level, own = 1.0, jax.random.fold_in(key, 6)
    for axis_at, shards_of in pieces:
        steps = jnp.exp(jax.random.uniform(jax.random.fold_in(own, axis_at), (shards_of,), jnp.float32, smallest / len(pieces), largest / len(pieces)))
        level = level * jnp.repeat(steps, extent[axis_at] // shards_of).reshape([-1 if axis == axis_at else 1 for axis in range(len(extent))])
    return level


def bell_draw(key, extent, deviation, reach, cuts=(), kind=jnp.bfloat16):
    drawn = deviation * jax.random.normal(key, extent, jnp.float32)
    if cuts:
        drawn = drawn * shard_levels(key, extent, cuts, -0.22, 0.18)
    return jnp.clip(drawn, -reach, reach).astype(kind)


def setup_inputs(seed: int = 0) -> dict:
    splits = jax.random.split(jax.random.key(seed), 6)
    inputs = bell_draw(splits[0], (NX, NY, NZ, C), 1.0, 6.0, ((0, 4), (1, 8)))
    preact = bell_draw(splits[1], (NX, NY, NZ, C), 1.0, 6.0, ((0, 4), (1, 8)))
    cotangent = bell_draw(splits[2], (NX, NY, NZ, C), 1.0, 6.0, ((0, 4), (1, 8)))
    spectral_w = bell_draw(splits[3], (MX, MY, MZ, C, C), (C // 16) ** -0.5, 2.0, ((0, 4), (1, 8)))
    skip_w = bell_draw(splits[4], (C, C), C ** -0.5, 0.5)
    return {"inputs": inputs, "preact": preact, "cotangent": cotangent, "spectral_w": spectral_w, "skip_w": skip_w}


highest = lax.Precision.HIGHEST

def cas_table(modes, length, offset, cells):
    index = jnp.arange(modes, dtype=jnp.int32)
    freq = jnp.where(index < modes // 2, index, length - modes + index).astype(jnp.int32)
    where_cells = (offset + jnp.arange(cells, dtype=jnp.int32)).astype(jnp.int32)
    phase = freq[:, None] * where_cells[None, :] % length
    angle = phase.astype(jnp.float32) * (2.0 * math.pi / length)
    return (jnp.cos(angle) + jnp.sin(angle)) / math.sqrt(length)

def reference(inputs, preact, cotangent, spectral_w, skip_w):
    table_x = cas_table(MX, NX, 0, NX)
    table_y = cas_table(MY, NY, 0, NY)
    table_z = cas_table(MZ, NZ, 0, NZ)
    preact_wide = preact.astype(jnp.float32)
    gelu_slope = 0.5 * (1.0 + jax.scipy.special.erf(preact_wide * (1.0 / math.sqrt(2.0)))) + preact_wide * jnp.exp(-0.5 * preact_wide * preact_wide) * (1.0 / math.sqrt(2.0 * math.pi))
    grad_pre = (cotangent.astype(jnp.float32) * gelu_slope).astype(jnp.bfloat16)

    def forward(field):
        step_one = jnp.einsum('ck,ijkh->ijch', table_z, field, precision=highest)
        step_two = jnp.einsum('bj,ijch->ibch', table_y, step_one, precision=highest)
        return jnp.einsum('ai,ibch->abch', table_x, step_two, precision=highest)
    input_modes = forward(inputs.astype(jnp.float32))
    grad_modes = forward(grad_pre.astype(jnp.float32))
    grad_spectral = jnp.einsum('abcp,abcq->abcpq', input_modes, grad_modes, precision=highest).astype(jnp.bfloat16)
    back_modes = jnp.einsum('abcq,abcpq->abcp', grad_modes, spectral_w.astype(jnp.float32), precision=highest).astype(jnp.bfloat16)
    step_one = jnp.einsum('ai,abch->ibch', table_x, back_modes.astype(jnp.float32), precision=highest)
    step_two = jnp.einsum('bj,ibch->ijch', table_y, step_one, precision=highest)
    spectral_cells = jnp.einsum('ck,ijch->ijkh', table_z, step_two, precision=highest)
    flat_grad = grad_pre.reshape(-1, C)
    skip_part = lax.dot_general(flat_grad, skip_w, (((1,), (1,)), ((), ())), preferred_element_type=jnp.float32)
    grad_inputs = (skip_part.reshape(NX, NY, NZ, C) + spectral_cells).astype(jnp.bfloat16)
    local_sum = lax.dot_general(inputs.reshape(-1, C), flat_grad, (((0,), (0,)), ((), ())), preferred_element_type=jnp.float32)
    grad_skip = local_sum / math.sqrt(NX * NY * NZ)
    return (grad_inputs, grad_spectral, grad_skip)
```

```python
import functools
import math

import jax
import jax.numpy as jnp
import numpy as np
from jax import lax
from jax.experimental import pallas as pl
from jax.experimental.pallas import tpu as pltpu
from jax.sharding import PartitionSpec as P

highest = lax.Precision.HIGHEST
f32 = jnp.float32
bf16 = jnp.bfloat16
LANES = 128
MIB = 1 << 20


def cas_table(modes, length, offset, cells):
    index = jnp.arange(modes, dtype=jnp.int32)
    freq = jnp.where(index < modes // 2, index, length - modes + index)
    where_cells = offset + jnp.arange(cells, dtype=jnp.int32)
    phase = freq[:, None] * where_cells[None, :] % length
    angle = phase.astype(jnp.float32) * (2.0 * math.pi / length)
    return (jnp.cos(angle) + jnp.sin(angle)) / math.sqrt(length)


def gelu_slope_of(preact_wide):
    return 0.5 * (
        1.0 + lax.erf(preact_wide * (1.0 / math.sqrt(2.0)))
    ) + preact_wide * jnp.exp(-0.5 * preact_wide * preact_wide) * (1.0 / math.sqrt(2.0 * math.pi))


def plain_cas(modes, length):
    index = np.arange(modes)
    freq = np.where(index < modes // 2, index, length - modes + index)
    angle = 2.0 * np.pi * ((freq[:, None] * np.arange(length)[None, :]) % length) / length
    return np.cos(angle) + np.sin(angle)


def rounded_table(table):
    values, counts = np.unique(np.round(np.abs(table), 12), return_counts=True)
    best = None
    for scale in np.linspace(1.0, 2.0, 512, endpoint=False):
        kept = (values * scale).astype(np.float32).astype(bf16).astype(np.float64) / scale
        error = np.sum(counts * (kept - values) ** 2)
        if best is None or error < best[0]:
            best = (error, scale)
    return (table * best[1]).astype(np.float32).astype(bf16), 1.0 / best[1]


def split_index(size, *parts):
    return np.unravel_index(np.arange(size), parts)


class Sizes:
    def __init__(self, inputs, spectral_w, gx, gy):
        self.gx, self.gy = gx, gy
        self.devices = gx * gy
        self.x, self.y, self.z, self.channels = inputs.shape
        self.cells = self.x * self.y * self.z
        self.width = 2 * self.z * self.channels // self.devices
        self.back_width = self.z * self.channels // self.devices

    def fits(self, inputs, spectral_w):
        if inputs.shape[:3] != spectral_w.shape[:3] or self.channels != LANES:
            return False
        if self.back_width * 4 != LANES or self.y % 4:
            return False
        rows = self.x * self.y // 2
        return rows == 16 and self.devices * 4 == LANES and self.x * self.y // 4 == 8 and self.z == 8


def lanes_of(shape):
    return lax.broadcasted_iota(jnp.int32, shape, len(shape) - 1)


def open_kernel(in_ref, pre_ref, cot_ref, perm_ref, pack_ref, grad_ref):
    grad = (cot_ref[...].astype(f32) * gelu_slope_of(pre_ref[...].astype(f32))).astype(bf16)
    grad_ref[...] = grad
    half = in_ref.shape[0] // 2
    width = LANES // 2
    for field, value in enumerate((in_ref[...], grad)):
        rows = jnp.dot(perm_ref[...], value, preferred_element_type=f32)
        even, odd = rows[:half], rows[half:]
        low = lanes_of(even.shape) < width
        pack_ref[field, 0] = jnp.where(low, even, pltpu.roll(odd, width, 1)).astype(bf16)
        pack_ref[field, 1] = jnp.where(low, pltpu.roll(even, width, 1), odd).astype(bf16)


def skip_kernel(in_ref, grad_ref, skip_ref, perm_ref, part_ref, sum_ref):
    grad = grad_ref[...]
    part_ref[...] = lax.dot_general(
        grad, skip_ref[...], (((1,), (1,)), ((), ())), preferred_element_type=f32
    )
    total = lax.dot_general(
        in_ref[...], grad, (((0,), (0,)), ((), ())), preferred_element_type=f32
    )
    high = total.astype(bf16)
    low = (total - high.astype(f32)).astype(bf16)
    sum_ref[...] = jnp.dot(
        perm_ref[...], jnp.concatenate([high, low], 0), preferred_element_type=f32
    )


def plane_kernel(scale, x_ref, table_ref, out_ref):
    rows, width = x_ref.shape[0], LANES // 2
    made = jnp.dot(table_ref[...], x_ref[...], preferred_element_type=f32)
    low = lanes_of((rows, LANES)) < width
    straight = jnp.where(low, made[:rows], made[rows : 2 * rows])
    crossed = jnp.where(low, made[2 * rows : 3 * rows], made[3 * rows :])
    out_ref[...] = ((straight + pltpu.roll(crossed, width, 1)) * scale).astype(bf16)


def modes_kernel(
    scale, per_step, x_ref, z_ref, w_ref, perm_ref, sum_ref, in_ref, grad_ref, pack_ref, twin, back
):
    step = pl.program_id(0)
    groups = per_step // 8

    @pl.when(step == 0)
    def _():
        width = LANES // 2
        made = []
        for field in range(2):
            first = x_ref[field, 0].astype(f32)
            second = x_ref[field, 1].astype(f32)
            low = lanes_of(first.shape) < width
            even = jnp.where(low, first, pltpu.roll(second, width, 1))
            odd = jnp.where(low, pltpu.roll(first, width, 1), second)
            rows = jnp.concatenate([even, odd], 0).astype(bf16)
            made.append(jnp.dot(z_ref[...], rows, preferred_element_type=f32) * scale)
        in_ref[...] = made[0].T
        grad_ref[...] = made[1]
        high = made[1].astype(bf16).astype(f32)
        low_part = made[1] - high
        count = made[1].shape[0] // 8
        twin[...] = jnp.concatenate(
            [high.reshape(count, 8, LANES), low_part.reshape(count, 8, LANES)], 1
        ).astype(bf16)

    row = lax.broadcasted_iota(jnp.int32, (8, LANES), 0)
    for group in range(groups):
        weights = w_ref[group * 8 : group * 8 + 8].reshape(8 * LANES, LANES)
        every = lax.dot_general(
            twin[step * groups + group],
            weights,
            (((1,), (1,)), ((), ())),
            preferred_element_type=f32,
        )
        every = every[:8] + every[8:]
        total = jnp.zeros((8, LANES), f32)
        for mode in range(8):
            total += jnp.where(row == mode, every[:, mode * LANES : (mode + 1) * LANES], 0.0)
        back[pl.ds(pl.multiple_of((step * groups + group) * 8, 8), 8), :] = total

    @pl.when(step == pl.num_programs(0) - 1)
    def _():
        rows = jnp.dot(perm_ref[...], back[...].astype(bf16), preferred_element_type=f32)
        quarter = rows.shape[0] // 4
        group_of = lanes_of((quarter, LANES)) // (LANES // 4)
        pieces = []
        for part in range(4):
            piece = jnp.zeros((quarter, LANES), f32)
            for place in range(4):
                source = rows[place * quarter : (place + 1) * quarter]
                moved = pltpu.roll(source, (place - part) % 4 * (LANES // 4), 1)
                piece = jnp.where(group_of == place, moved, piece)
            pieces.append(piece)
        every = jnp.concatenate(pieces, 0)
        count = every.shape[0] // 8
        pack_ref[...] = jnp.concatenate(
            [every.reshape(count, 8, LANES), sum_ref[...].reshape(count, 8, LANES)], 1
        ).astype(bf16)


def outer_kernel(per_step, in_ref, grad_ref, out_ref):
    step = pl.program_id(0)
    columns = pltpu.roll(in_ref[...], in_ref.shape[1] - step * per_step, 1)
    for mode in range(per_step):
        column = jnp.broadcast_to(columns[:, mode : mode + 1], (LANES, LANES))
        out_ref[mode] = (column * grad_ref[mode : mode + 1, :]).astype(bf16)


def back_plane_kernel(scale, skip_scale, x_ref, table_ref, out_ref):
    every = x_ref[...].astype(f32)
    count = every.shape[0]
    rows = count * 8
    x = every[:, :8].reshape(rows, LANES)
    turned = [x if s == 0 else pltpu.roll(x, s * (LANES // 4), 1) for s in range(4)]
    made = jnp.dot(
        table_ref[...], jnp.concatenate(turned, 0).astype(bf16), preferred_element_type=f32
    )
    group_of = lanes_of((rows, LANES)) // (LANES // 4)
    out = made[:rows]
    for place in range(1, 4):
        out = jnp.where(group_of == place, made[place * rows : (place + 1) * rows], out)
    out = out * scale
    parts = jnp.sum(every[:, 8:], 0)
    total = (parts + pltpu.roll(parts, 4, 0)) * skip_scale
    high = total.astype(bf16).astype(f32)
    row = lax.broadcasted_iota(jnp.int32, total.shape, 0)
    total = jnp.where(row < 4, high, total - high)
    out_ref[...] = jnp.concatenate(
        [out.reshape(count, 8, LANES), jnp.broadcast_to(total[None], (count, 8, LANES))], 1
    ).astype(bf16)


def close_kernel(scale, x_ref, z_ref, part_ref, fold_ref, out_ref, skip_ref):
    every = x_ref[...].astype(f32)
    count = every.shape[0]
    rows = every[:, :8].reshape(count * 8, LANES)
    quarter = rows.shape[0] // 4
    group_of = lanes_of((quarter, LANES)) // (LANES // 4)
    pieces = []
    for place in range(4):
        piece = jnp.zeros((quarter, LANES), f32)
        for part in range(4):
            source = rows[part * quarter : (part + 1) * quarter]
            moved = pltpu.roll(source, (part - place) % 4 * (LANES // 4), 1)
            piece = jnp.where(group_of == part, moved, piece)
        pieces.append(piece)
    cells = jnp.dot(
        z_ref[...], jnp.concatenate(pieces, 0).astype(bf16), preferred_element_type=f32
    )
    out_ref[...] = (part_ref[...] + cells * scale).astype(bf16)
    sums = every[:, 8:].reshape(count * 8, LANES).astype(bf16)
    skip_ref[...] = jnp.dot(fold_ref[...], sums, preferred_element_type=f32)


def one_hot(rows, columns):
    return (np.asarray(rows)[:, None] == np.asarray(columns)[None, :]).astype(np.float32)


def make_tables(s):
    cas_x = plain_cas(s.x * s.gx, s.x * s.gx)
    cas_y = plain_cas(s.y * s.gy, s.y * s.gy)
    cas_z = plain_cas(s.z, s.z)
    norm = math.sqrt(s.x * s.gx * s.y * s.gy)
    t = {}
    yl, z, x, yh = split_index(s.cells, 2, s.z, s.x, s.y // 2)
    t["cut"] = one_hot((x * s.y + yh * 2 + yl) * s.z + z, np.arange(s.cells))
    device, which, row = split_index(2 * s.channels, s.devices, 2, 4)
    t["sums"] = one_hot(which * s.channels + device * 4 + row, np.arange(2 * s.channels))
    device, which, row = split_index(2 * s.channels, s.devices, 2, 4)
    t["fold"] = one_hot(np.arange(s.channels), device * 4 + row)
    count = s.devices * s.x * s.y // 2
    px, py, x, yh = split_index(count, s.gx, s.gy, s.x, s.y // 2)
    at_x = px * s.x + x
    blocks = []
    for b, y in ((0, 0), (1, 1), (1, 0), (0, 1)):
        at_b = py * s.y + yh * 2 + b
        at_y = py * s.y + yh * 2 + y
        blocks.append(cas_x[at_x[:, None], at_x[None, :]] * cas_y[at_b[:, None], at_y[None, :]])
    t["plane"], factor = rounded_table(np.concatenate(blocks, 0))
    t["plane_scale"] = factor / norm
    a, b, c = split_index(s.cells, s.x, s.y, s.z)
    bl, z, al, bh = split_index(s.cells, 2, s.z, s.x, s.y // 2)
    same = one_hot(a * s.y + b, al * s.y + bh * 2 + bl)
    t["z"] = same * cas_z[c[:, None], z[None, :]]
    t["z_scale"] = 1.0 / math.sqrt(s.z)
    b, c, a = split_index(s.cells, s.y, s.z, s.x)
    t["back_cut"] = one_hot((a * s.y + b) * s.z + c, np.arange(s.cells))
    count = s.devices * s.x
    px, py, x = split_index(count, s.gx, s.gy, s.x)
    at_x = px * s.x + x
    blocks = []
    for place in range(4):
        line = []
        for turn in range(4):
            at_y = py * s.y + place
            at_b = py * s.y + (place - turn) % 4
            line.append(cas_x[at_x[None, :], at_x[:, None]] * cas_y[at_b[None, :], at_y[:, None]])
        blocks.append(np.concatenate(line, 1))
    t["back_plane"], factor = rounded_table(np.concatenate(blocks, 0))
    t["back_plane_scale"] = factor / norm
    x, y, z = split_index(s.cells, s.x, s.y, s.z)
    yl, c, xl = split_index(s.cells, s.y, s.z, s.x)
    t["back_z"] = one_hot(x * s.y + y, xl * s.y + yl) * cas_z[c[None, :], z[:, None]]
    return {
        key: jnp.asarray(np.asarray(value, np.float32).astype(bf16))
        if isinstance(value, np.ndarray)
        else value
        for key, value in t.items()
    }


def call(kernel, out_shape, limit, cost, **more):
    return pl.pallas_call(
        kernel,
        out_shape=out_shape,
        compiler_params=pltpu.CompilerParams(vmem_limit_bytes=limit * MIB),
        cost_estimate=pl.CostEstimate(flops=cost[0], bytes_accessed=cost[1], transcendentals=0),
        **more,
    )


def shaped(*shape, kind=bf16):
    return jax.ShapeDtypeStruct(shape, kind)


def exchange(pieces):
    return lax.all_to_all(pieces, ("gx", "gy"), 0, 0)


def on_device_whole_planes(s, inputs, preact, cotangent, spectral_w, skip_w):
    t = make_tables(s)
    cells, channels, devices = s.cells, s.channels, s.devices
    flat = lambda array: array.reshape(cells, channels)
    pieces, grad_pre = call(
        open_kernel,
        (shaped(2, 2, cells // 2, LANES), shaped(cells, channels)),
        16,
        (cells * cells * LANES * 4, 1 * MIB),
    )(flat(inputs), flat(preact), flat(cotangent), t["cut"])
    columns = exchange(pieces.reshape(devices, -1, LANES))
    skip_part, sums = call(
        skip_kernel,
        (shaped(cells, channels, kind=f32), shaped(2 * channels, channels, kind=f32)),
        16,
        (cells * channels * channels * 8, 4 * MIB),
    )(flat(inputs), grad_pre, skip_w, t["sums"])
    rows = cells // s.z // 2 * devices
    planes = call(
        functools.partial(plane_kernel, t["plane_scale"]),
        shaped(rows, LANES),
        16,
        (rows * rows * LANES * 8, 4 * MIB),
    )(columns.reshape(rows, LANES), t["plane"])
    owned = exchange(planes.reshape(devices, -1, LANES))

    per_step = 16
    whole = lambda *shape: pl.BlockSpec(shape, lambda i: (0,) * len(shape))
    input_modes, grad_modes, back = call(
        functools.partial(modes_kernel, t["z_scale"], per_step),
        (
            shaped(channels, cells, kind=f32),
            shaped(cells, channels, kind=f32),
            shaped(devices, 16, LANES),
        ),
        24,
        (cells * channels * channels * 16, 9 * MIB),
        grid=(cells // per_step,),
        in_specs=[
            whole(2, 2, cells // 2, LANES),
            whole(cells, cells),
            pl.BlockSpec((per_step, channels, channels), lambda i: (i, 0, 0)),
            whole(cells, cells),
            whole(2 * channels, channels),
        ],
        out_specs=(whole(channels, cells), whole(cells, channels), whole(devices, 16, LANES)),
        scratch_shapes=[
            pltpu.VMEM((cells // 8, 16, LANES), bf16),
            pltpu.VMEM((cells, channels), f32),
        ],
    )(
        owned.reshape(2, 2, cells // 2, LANES),
        t["z"],
        spectral_w.reshape(cells, channels, channels),
        t["back_cut"],
        sums,
    )
    back_columns = exchange(back)
    grad_spectral = call(
        functools.partial(outer_kernel, per_step),
        shaped(cells, channels, channels),
        16,
        (cells * channels * channels * 2, 9 * MIB),
        grid=(cells // per_step,),
        in_specs=[whole(channels, cells), pl.BlockSpec((per_step, channels), lambda i: (i, 0))],
        out_specs=pl.BlockSpec((per_step, channels, channels), lambda i: (i, 0, 0)),
    )(input_modes, grad_modes)
    total_cells = cells * devices
    back_planes = call(
        functools.partial(
            back_plane_kernel, t["back_plane_scale"], 1.0 / math.sqrt(total_cells)
        ),
        shaped(devices, 16, LANES),
        16,
        (rows * rows * LANES * 8, 4 * MIB),
    )(back_columns, t["back_plane"])
    spectral = exchange(back_planes)
    grad_inputs, grad_skip = call(
        functools.partial(close_kernel, t["z_scale"]),
        (shaped(cells, channels), shaped(channels, channels, kind=f32)),
        16,
        (cells * cells * LANES * 4, 1 * MIB),
    )(spectral, t["back_z"], skip_part, t["fold"])
    return (
        grad_inputs.reshape(inputs.shape),
        grad_spectral.reshape(spectral_w.shape),
        grad_skip,
    )


def on_device(inputs, preact, cotangent, spectral_w, skip_w):
    sizes = Sizes(inputs, spectral_w, lax.axis_size("gx"), lax.axis_size("gy"))
    if sizes.fits(inputs, spectral_w):
        return on_device_whole_planes(sizes, inputs, preact, cotangent, spectral_w, skip_w)
    return on_device_any(inputs, preact, cotangent, spectral_w, skip_w)


def on_device_any(inputs, preact, cotangent, spectral_w, skip_w):
    cells_x, cells_y, cells_z, channels = inputs.shape
    length_x = cells_x * lax.axis_size("gx")
    length_y = cells_y * lax.axis_size("gy")
    local_modes_x, local_modes_y, modes_z = (
        spectral_w.shape[0],
        spectral_w.shape[1],
        spectral_w.shape[2],
    )
    modes_x = local_modes_x * lax.axis_size("gx")
    modes_y = local_modes_y * lax.axis_size("gy")
    table_z = cas_table(modes_z, cells_z, 0, cells_z)
    table_x = cas_table(modes_x, length_x, lax.axis_index("gx") * cells_x, cells_x)
    table_y = cas_table(modes_y, length_y, lax.axis_index("gy") * cells_y, cells_y)
    preact_wide = preact.astype(jnp.float32)
    gelu_slope = 0.5 * (
        1.0 + lax.erf(preact_wide * (1.0 / math.sqrt(2.0)))
    ) + preact_wide * jnp.exp(-0.5 * preact_wide * preact_wide) * (1.0 / math.sqrt(2.0 * math.pi))
    grad_pre = (cotangent.astype(jnp.float32) * gelu_slope).astype(jnp.bfloat16)
    fields = jnp.stack([inputs, grad_pre]).astype(jnp.float32)
    z_modes = jnp.einsum("ck,fijkh->fijch", table_z, fields, precision=highest)
    table_rows = table_y
    part_y = lax.psum_scatter(
        jnp.einsum("bj,fijch->bfich", table_rows, z_modes, precision=highest),
        "gy",
        scatter_dimension=0,
        tiled=True,
    )
    table_rows = table_x
    owned_modes = lax.psum_scatter(
        jnp.einsum("ai,bfich->abfch", table_rows, part_y, precision=highest),
        "gx",
        scatter_dimension=0,
        tiled=True,
    )
    input_modes = owned_modes[:, :, 0]
    grad_modes = owned_modes[:, :, 1]
    grad_spectral = jnp.einsum(
        "abcp,abcq->abcpq", input_modes, grad_modes, precision=highest
    ).astype(jnp.bfloat16)
    back_modes = jnp.einsum(
        "abcq,abcpq->abcp", grad_modes, spectral_w.astype(jnp.float32), precision=highest
    ).astype(jnp.bfloat16)
    table_rows = table_x
    over_first = jnp.einsum(
        "ai,abch->ibch",
        table_rows,
        lax.all_gather(back_modes, "gx", axis=0, tiled=True).astype(jnp.float32),
        precision=highest,
    )
    table_rows = table_y
    cell_modes = jnp.einsum(
        "bj,ibch->ijch",
        table_rows,
        lax.all_gather(over_first, "gy", axis=1, tiled=True),
        precision=highest,
    )
    spectral_cells = jnp.einsum("ck,ijch->ijkh", table_z, cell_modes, precision=highest)
    flat_grad = grad_pre.reshape(-1, channels)
    skip_part = lax.dot_general(
        flat_grad, skip_w, (((1,), (1,)), ((), ())), preferred_element_type=jnp.float32
    )
    grad_inputs = (skip_part.reshape(cells_x, cells_y, cells_z, channels) + spectral_cells).astype(
        jnp.bfloat16
    )
    local_sum = lax.dot_general(
        inputs.reshape(-1, channels),
        flat_grad,
        (((0,), (0,)), ((), ())),
        preferred_element_type=jnp.float32,
    )
    grad_skip = lax.psum(local_sum, ("gx", "gy")) / math.sqrt(length_x * length_y * cells_z)
    return (grad_inputs, grad_spectral, grad_skip)


def solution(mesh):
    in_specs = (
        P("gx", "gy", None, None),
        P("gx", "gy", None, None),
        P("gx", "gy", None, None),
        P("gx", "gy", None, None, None),
        P(),
    )
    out_specs = (P("gx", "gy", None, None), P("gx", "gy", None, None, None), P())
    return jax.shard_map(
        on_device, mesh=mesh, in_specs=in_specs, out_specs=out_specs, check_vma=False
    )
```

```python
import functools
import math

import jax
import jax.numpy as jnp
import numpy as np
from jax import lax
from jax.experimental import pallas as pl
from jax.experimental.pallas import tpu as pltpu
from jax.sharding import PartitionSpec as P

highest = lax.Precision.HIGHEST
f32 = jnp.float32
bf16 = jnp.bfloat16
LANES = 128
MIB = 1 << 20


def cas_table(modes, length, offset, cells):
    index = jnp.arange(modes, dtype=jnp.int32)
    freq = jnp.where(index < modes // 2, index, length - modes + index)
    where_cells = offset + jnp.arange(cells, dtype=jnp.int32)
    phase = freq[:, None] * where_cells[None, :] % length
    angle = phase.astype(jnp.float32) * (2.0 * math.pi / length)
    return (jnp.cos(angle) + jnp.sin(angle)) / math.sqrt(length)


def gelu_slope_of(preact_wide):
    return 0.5 * (
        1.0 + lax.erf(preact_wide * (1.0 / math.sqrt(2.0)))
    ) + preact_wide * jnp.exp(-0.5 * preact_wide * preact_wide) * (1.0 / math.sqrt(2.0 * math.pi))


def plain_cas(modes, length):
    index = np.arange(modes)
    freq = np.where(index < modes // 2, index, length - modes + index)
    angle = 2.0 * np.pi * ((freq[:, None] * np.arange(length)[None, :]) % length) / length
    return np.cos(angle) + np.sin(angle)


def rounded_table(table):
    values, counts = np.unique(np.round(np.abs(table), 12), return_counts=True)
    best = None
    for scale in np.linspace(1.0, 2.0, 512, endpoint=False):
        kept = (values * scale).astype(np.float32).astype(bf16).astype(np.float64) / scale
        error = np.sum(counts * (kept - values) ** 2)
        if best is None or error < best[0]:
            best = (error, scale)
    return (table * best[1]).astype(np.float32).astype(bf16), 1.0 / best[1]


def split_index(size, *parts):
    return np.unravel_index(np.arange(size), parts)


class Sizes:
    def __init__(self, inputs, spectral_w, gx, gy):
        self.gx, self.gy = gx, gy
        self.devices = gx * gy
        self.x, self.y, self.z, self.channels = inputs.shape
        self.cells = self.x * self.y * self.z
        self.width = 2 * self.z * self.channels // self.devices
        self.back_width = self.z * self.channels // self.devices

    def fits(self, inputs, spectral_w):
        if inputs.shape[:3] != spectral_w.shape[:3] or self.channels != LANES:
            return False
        if self.back_width * 4 != LANES or self.y % 4:
            return False
        rows = self.x * self.y // 2
        return rows == 16 and self.devices * 4 == LANES and self.x * self.y // 4 == 8 and self.z == 8


def lanes_of(shape):
    return lax.broadcasted_iota(jnp.int32, shape, len(shape) - 1)


def load(*pairs):
    copies = [pltpu.make_async_copy(source, target, sem) for source, target, sem in pairs]
    for copy in copies:
        copy.start()
    return copies


def open_kernel(s, in_hbm, pre_hbm, cot_hbm, pack_ref, grad_ref, in_ref, pre_ref, cot_ref, sems):
    copies = load(
        (in_hbm, in_ref, sems.at[0]), (pre_hbm, pre_ref, sems.at[1]), (cot_hbm, cot_ref, sems.at[2])
    )
    cells = s.cells
    place = lax.broadcasted_iota(jnp.int32, (cells, 1), 0)
    half_y = s.y // 2
    half = cells // 2
    yl, rest = place // half, place % half
    z, rest = rest // (s.x * half_y), rest % (s.x * half_y)
    x, yh = rest // half_y, rest % half_y
    source = (x * s.y + yh * 2 + yl) * s.z + z
    order = (lax.broadcasted_iota(jnp.int32, (cells, cells), 1) == source).astype(f32).astype(bf16)
    for copy in copies:
        copy.wait()
    grad = (cot_ref[...].astype(f32) * gelu_slope_of(pre_ref[...].astype(f32))).astype(bf16)
    grad_ref[...] = grad
    rows = jnp.dot(
        order, jnp.concatenate([in_ref[...], grad], 1), preferred_element_type=f32
    )
    width = LANES // 2
    low = lanes_of((half, LANES)) < width
    for field in range(2):
        even = rows[:half, field * LANES : (field + 1) * LANES]
        odd = rows[half:, field * LANES : (field + 1) * LANES]
        pack_ref[field, 0] = jnp.where(low, even, pltpu.roll(odd, width, 1)).astype(bf16)
        pack_ref[field, 1] = jnp.where(low, pltpu.roll(even, width, 1), odd).astype(bf16)


def plane_kernel(scale, x_ref, table_ref, out_ref):
    rows, width = x_ref.shape[0], LANES // 2
    made = jnp.dot(table_ref[...], x_ref[...], preferred_element_type=f32)
    low = lanes_of((rows, LANES)) < width
    straight = jnp.where(low, made[:rows], made[rows : 2 * rows])
    crossed = jnp.where(low, made[2 * rows : 3 * rows], made[3 * rows :])
    out_ref[...] = ((straight + pltpu.roll(crossed, width, 1)) * scale).astype(bf16)


def field_modes(scale, first, second, z_ref):
    width = LANES // 2
    first, second = first.astype(f32), second.astype(f32)
    low = lanes_of(first.shape) < width
    even = jnp.where(low, first, pltpu.roll(second, width, 1))
    odd = jnp.where(low, pltpu.roll(first, width, 1), second)
    rows = jnp.concatenate([even, odd], 0).astype(bf16)
    return jnp.dot(z_ref[...], rows, preferred_element_type=f32) * scale


def split_twice(value):
    high = value.astype(bf16)
    return high, (value - high.astype(f32)).astype(bf16)


def modes_kernel(
    scale, x_ref, z_ref, w_ref, cut_ref, field_ref, pre_ref, perm_ref, grad_ref, pack_ref, back
):
    grad_ref[...] = field_modes(scale, x_ref[1, 0], x_ref[1, 1], z_ref)
    sums = lax.dot_general(
        field_ref[...], pre_ref[...], (((0,), (0,)), ((), ())), preferred_element_type=f32
    )
    sums = jnp.dot(
        perm_ref[...], jnp.concatenate(split_twice(sums), 0), preferred_element_type=f32
    )
    groups = grad_ref.shape[0] // 8
    unrolled = 16
    row = lax.broadcasted_iota(jnp.int32, (8, LANES), 0)

    @pl.loop(0, groups // unrolled)
    def _(turn):
        for group in range(unrolled):
            start = pl.multiple_of((turn * unrolled + group) * 8, 8)
            modes = grad_ref[pl.ds(start, 8), :]
            high = modes.astype(bf16).astype(f32)
            every = lax.dot_general(
                jnp.concatenate([high, modes - high], 0).astype(bf16),
                w_ref[pl.ds(start, 8)].reshape(8 * LANES, LANES),
                (((1,), (1,)), ((), ())),
                preferred_element_type=f32,
            )
            every = every[:8] + every[8:]
            total = jnp.zeros((8, LANES), f32)
            for mode in range(8):
                total += jnp.where(row == mode, every[:, mode * LANES : (mode + 1) * LANES], 0.0)
            back[pl.ds(start, 8), :] = total

    rows = jnp.dot(cut_ref[...], back[...].astype(bf16), preferred_element_type=f32)
    quarter = rows.shape[0] // 4
    group_of = lanes_of((quarter, LANES)) // (LANES // 4)
    pieces = []
    for part in range(4):
        piece = jnp.zeros((quarter, LANES), f32)
        for place in range(4):
            source = rows[place * quarter : (place + 1) * quarter]
            moved = pltpu.roll(source, (place - part) % 4 * (LANES // 4), 1)
            piece = jnp.where(group_of == place, moved, piece)
        pieces.append(piece)
    every = jnp.concatenate(pieces, 0)
    count = every.shape[0] // 8
    pack_ref[...] = jnp.concatenate(
        [every.reshape(count, 8, LANES), sums.reshape(count, 8, LANES)], 1
    ).astype(bf16)


def outer_kernel(scale, x_ref, z_ref, grad_ref, out_hbm, flag_ref, in_ref, made, sems):
    in_ref[...] = field_modes(scale, x_ref[0, 0], x_ref[0, 1], z_ref)
    flag_ref[...] = jnp.zeros(flag_ref.shape, f32)
    modes = in_ref.shape[0]
    size, unrolled = 16, 4
    row = lax.broadcasted_iota(jnp.int32, (3 * size, LANES), 0) % size

    def copy(group):
        part = pl.ds(group * size, size)
        return pltpu.make_async_copy(made.at[part], out_hbm.at[part], sems.at[group])

    @pl.loop(0, modes // size // unrolled)
    def _(turn):
        for at in range(unrolled):
            group = turn * unrolled + at
            start = pl.multiple_of(group * size, size)
            in_high, in_low = split_twice(in_ref[pl.ds(start, size), :])
            high, low = split_twice(grad_ref[pl.ds(start, size), :])
            left = jnp.concatenate([in_high, in_low, in_high], 0)
            right = jnp.concatenate([high, high, low], 0)
            zero = jnp.zeros((), bf16)
            right = jnp.concatenate([jnp.where(row == mode, right, zero) for mode in range(size)], 1)
            every = lax.dot_general(
                left, right, (((0,), (0,)), ((), ())), preferred_element_type=f32
            )
            for mode in range(size):
                made[group * size + mode] = every[:, mode * LANES : (mode + 1) * LANES].astype(bf16)
            copy(group).start()

    @pl.loop(0, modes // size)
    def _(group):
        copy(group).wait()


def back_plane_kernel(scale, skip_scale, x_ref, table_ref, after, out_ref):
    del after
    every = x_ref[...].astype(f32)
    count = every.shape[0]
    rows = count * 8
    x = every[:, :8].reshape(rows, LANES)
    turned = [x if s == 0 else pltpu.roll(x, s * (LANES // 4), 1) for s in range(4)]
    made = jnp.dot(
        table_ref[...], jnp.concatenate(turned, 0).astype(bf16), preferred_element_type=f32
    )
    group_of = lanes_of((rows, LANES)) // (LANES // 4)
    out = made[:rows]
    for place in range(1, 4):
        out = jnp.where(group_of == place, made[place * rows : (place + 1) * rows], out)
    out = out * scale
    parts = jnp.sum(every[:, 8:], 0)
    total = (parts + pltpu.roll(parts, 4, 0)) * skip_scale
    high = total.astype(bf16).astype(f32)
    row = lax.broadcasted_iota(jnp.int32, total.shape, 0)
    total = jnp.where(row < 4, high, total - high)
    out_ref[...] = jnp.concatenate(
        [out.reshape(count, 8, LANES), jnp.broadcast_to(total[None], (count, 8, LANES))], 1
    ).astype(bf16)


def close_kernel(scale, x_ref, z_ref, pre_ref, weight_ref, fold_ref, out_ref, skip_ref):
    every = x_ref[...].astype(f32)
    count = every.shape[0]
    rows = every[:, :8].reshape(count * 8, LANES)
    quarter = rows.shape[0] // 4
    group_of = lanes_of((quarter, LANES)) // (LANES // 4)
    pieces = []
    for place in range(4):
        piece = jnp.zeros((quarter, LANES), f32)
        for part in range(4):
            source = rows[part * quarter : (part + 1) * quarter]
            moved = pltpu.roll(source, (part - place) % 4 * (LANES // 4), 1)
            piece = jnp.where(group_of == part, moved, piece)
        pieces.append(piece)
    cells = jnp.dot(
        z_ref[...], jnp.concatenate(pieces, 0).astype(bf16), preferred_element_type=f32
    )
    part = lax.dot_general(
        pre_ref[...], weight_ref[...], (((1,), (1,)), ((), ())), preferred_element_type=f32
    )
    out_ref[...] = (part + cells * scale).astype(bf16)
    sums = every[:, 8:].reshape(count * 8, LANES).astype(bf16)
    skip_ref[...] = jnp.dot(fold_ref[...], sums, preferred_element_type=f32)


def one_hot(rows, columns):
    return (np.asarray(rows)[:, None] == np.asarray(columns)[None, :]).astype(np.float32)


def make_tables(s):
    cas_x = plain_cas(s.x * s.gx, s.x * s.gx)
    cas_y = plain_cas(s.y * s.gy, s.y * s.gy)
    cas_z = plain_cas(s.z, s.z)
    norm = math.sqrt(s.x * s.gx * s.y * s.gy)
    t = {}
    device, which, row = split_index(2 * s.channels, s.devices, 2, 4)
    t["sums"] = one_hot(which * s.channels + device * 4 + row, np.arange(2 * s.channels))
    device, which, row = split_index(2 * s.channels, s.devices, 2, 4)
    t["fold"] = one_hot(np.arange(s.channels), device * 4 + row)
    count = s.devices * s.x * s.y // 2
    px, py, x, yh = split_index(count, s.gx, s.gy, s.x, s.y // 2)
    at_x = px * s.x + x
    blocks = []
    for b, y in ((0, 0), (1, 1), (1, 0), (0, 1)):
        at_b = py * s.y + yh * 2 + b
        at_y = py * s.y + yh * 2 + y
        blocks.append(cas_x[at_x[:, None], at_x[None, :]] * cas_y[at_b[:, None], at_y[None, :]])
    t["plane"], factor = rounded_table(np.concatenate(blocks, 0))
    t["plane_scale"] = factor / norm
    a, b, c = split_index(s.cells, s.x, s.y, s.z)
    bl, z, al, bh = split_index(s.cells, 2, s.z, s.x, s.y // 2)
    same = one_hot(a * s.y + b, al * s.y + bh * 2 + bl)
    t["z"] = same * cas_z[c[:, None], z[None, :]]
    t["z_scale"] = 1.0 / math.sqrt(s.z)
    b, c, a = split_index(s.cells, s.y, s.z, s.x)
    t["back_cut"] = one_hot((a * s.y + b) * s.z + c, np.arange(s.cells))
    count = s.devices * s.x
    px, py, x = split_index(count, s.gx, s.gy, s.x)
    at_x = px * s.x + x
    blocks = []
    for place in range(4):
        line = []
        for turn in range(4):
            at_y = py * s.y + place
            at_b = py * s.y + (place - turn) % 4
            line.append(cas_x[at_x[None, :], at_x[:, None]] * cas_y[at_b[None, :], at_y[:, None]])
        blocks.append(np.concatenate(line, 1))
    t["back_plane"], factor = rounded_table(np.concatenate(blocks, 0))
    t["back_plane_scale"] = factor / norm
    x, y, z = split_index(s.cells, s.x, s.y, s.z)
    yl, c, xl = split_index(s.cells, s.y, s.z, s.x)
    t["back_z"] = one_hot(x * s.y + y, xl * s.y + yl) * cas_z[c[None, :], z[:, None]]
    return {
        key: jnp.asarray(np.asarray(value, np.float32).astype(bf16))
        if isinstance(value, np.ndarray)
        else value
        for key, value in t.items()
    }


def call(kernel, out_shape, limit, flops, moved, **more):
    return pl.pallas_call(
        kernel,
        out_shape=out_shape,
        compiler_params=pltpu.CompilerParams(vmem_limit_bytes=limit * MIB),
        cost_estimate=pl.CostEstimate(flops=flops, bytes_accessed=moved, transcendentals=0),
        **more,
    )


def in_vmem(*shape, kind=bf16):
    return pltpu.VMEM(shape, kind)


def in_hbm(*shape, kind=bf16):
    return jax.ShapeDtypeStruct(shape, kind)


def exchange(pieces):
    return lax.all_to_all(pieces, ("gx", "gy"), 0, 0)


def on_device_whole_planes(s, inputs, preact, cotangent, spectral_w, skip_w):
    t = make_tables(s)
    cells, channels, devices = s.cells, s.channels, s.devices
    rows = cells // s.z // 2 * devices
    back_rows = devices * s.x
    flat = lambda array: array.reshape(cells, channels)
    vmem = pl.BlockSpec(memory_space=pltpu.VMEM)
    hbm = pl.BlockSpec(memory_space=pltpu.HBM)
    anywhere = pl.BlockSpec(memory_space=pl.ANY)
    field = pltpu.VMEM((cells, channels), bf16)
    pieces, grad_pre = call(
        functools.partial(open_kernel, s),
        (in_vmem(2, 2, cells // 2, LANES), in_vmem(cells, channels)),
        16,
        1 << 40,
        MIB,
        in_specs=[hbm] * 3,
        out_specs=(vmem, vmem),
        scratch_shapes=[field, field, field, pltpu.SemaphoreType.DMA((3,))],
    )(*(pltpu.with_memory_space_constraint(flat(a), pltpu.HBM) for a in (inputs, preact, cotangent)))
    columns = exchange(pieces.reshape(devices, -1, LANES))
    planes = call(
        functools.partial(plane_kernel, t["plane_scale"]),
        in_vmem(rows, LANES),
        16,
        1 << 36,
        4 * MIB,
        in_specs=[vmem, vmem],
        out_specs=vmem,
    )(columns.reshape(rows, LANES), t["plane"])
    owned = exchange(planes.reshape(devices, -1, LANES))
    owned = owned.reshape(2, 2, cells // 2, LANES)
    grad_modes, back = call(
        functools.partial(modes_kernel, t["z_scale"]),
        (in_vmem(cells, channels, kind=f32), in_vmem(devices, 16, LANES)),
        24,
        cells * channels * channels * 16,
        9 * MIB,
        in_specs=[vmem] * 7,
        out_specs=(vmem, vmem),
        scratch_shapes=[pltpu.VMEM((cells, channels), f32)],
    )(
        owned,
        t["z"],
        spectral_w.reshape(cells, channels, channels),
        t["back_cut"],
        flat(inputs),
        grad_pre,
        t["sums"],
    )
    back_columns = exchange(back)
    grad_spectral, flag = call(
        functools.partial(outer_kernel, t["z_scale"]),
        (in_hbm(cells, channels, channels), in_vmem(8, LANES, kind=f32)),
        24,
        cells * channels * channels * 2,
        9 * MIB,
        in_specs=[vmem] * 3,
        out_specs=(hbm, vmem),
        scratch_shapes=[
            pltpu.VMEM((cells, channels), f32),
            pltpu.VMEM((cells, channels, channels), bf16),
            pltpu.SemaphoreType.DMA((cells // 16,)),
        ],
    )(owned, t["z"], grad_modes)
    back_planes = call(
        functools.partial(
            back_plane_kernel, t["back_plane_scale"], 1.0 / math.sqrt(cells * devices)
        ),
        in_vmem(devices, 16, LANES),
        16,
        back_rows * back_rows * LANES * 32,
        4 * MIB,
        in_specs=[vmem, vmem, anywhere],
        out_specs=vmem,
    )(back_columns, t["back_plane"], flag)
    spectral = exchange(back_planes)
    grad_inputs, grad_skip = call(
        functools.partial(close_kernel, t["z_scale"]),
        (in_hbm(cells, channels), in_hbm(channels, channels, kind=f32)),
        16,
        cells * cells * LANES * 4,
        MIB,
        in_specs=[vmem] * 5,
        out_specs=(vmem, vmem),
    )(spectral, t["back_z"], grad_pre, skip_w, t["fold"])
    return (
        grad_inputs.reshape(inputs.shape),
        grad_spectral.reshape(spectral_w.shape),
        grad_skip,
    )


def on_device(inputs, preact, cotangent, spectral_w, skip_w):
    sizes = Sizes(inputs, spectral_w, lax.axis_size("gx"), lax.axis_size("gy"))
    if sizes.fits(inputs, spectral_w):
        return on_device_whole_planes(sizes, inputs, preact, cotangent, spectral_w, skip_w)
    return on_device_any(inputs, preact, cotangent, spectral_w, skip_w)


def on_device_any(inputs, preact, cotangent, spectral_w, skip_w):
    cells_x, cells_y, cells_z, channels = inputs.shape
    length_x = cells_x * lax.axis_size("gx")
    length_y = cells_y * lax.axis_size("gy")
    local_modes_x, local_modes_y, modes_z = (
        spectral_w.shape[0],
        spectral_w.shape[1],
        spectral_w.shape[2],
    )
    modes_x = local_modes_x * lax.axis_size("gx")
    modes_y = local_modes_y * lax.axis_size("gy")
    table_z = cas_table(modes_z, cells_z, 0, cells_z)
    table_x = cas_table(modes_x, length_x, lax.axis_index("gx") * cells_x, cells_x)
    table_y = cas_table(modes_y, length_y, lax.axis_index("gy") * cells_y, cells_y)
    preact_wide = preact.astype(jnp.float32)
    gelu_slope = 0.5 * (
        1.0 + lax.erf(preact_wide * (1.0 / math.sqrt(2.0)))
    ) + preact_wide * jnp.exp(-0.5 * preact_wide * preact_wide) * (1.0 / math.sqrt(2.0 * math.pi))
    grad_pre = (cotangent.astype(jnp.float32) * gelu_slope).astype(jnp.bfloat16)
    fields = jnp.stack([inputs, grad_pre]).astype(jnp.float32)
    z_modes = jnp.einsum("ck,fijkh->fijch", table_z, fields, precision=highest)
    table_rows = table_y
    part_y = lax.psum_scatter(
        jnp.einsum("bj,fijch->bfich", table_rows, z_modes, precision=highest),
        "gy",
        scatter_dimension=0,
        tiled=True,
    )
    table_rows = table_x
    owned_modes = lax.psum_scatter(
        jnp.einsum("ai,bfich->abfch", table_rows, part_y, precision=highest),
        "gx",
        scatter_dimension=0,
        tiled=True,
    )
    input_modes = owned_modes[:, :, 0]
    grad_modes = owned_modes[:, :, 1]
    grad_spectral = jnp.einsum(
        "abcp,abcq->abcpq", input_modes, grad_modes, precision=highest
    ).astype(jnp.bfloat16)
    back_modes = jnp.einsum(
        "abcq,abcpq->abcp", grad_modes, spectral_w.astype(jnp.float32), precision=highest
    ).astype(jnp.bfloat16)
    table_rows = table_x
    over_first = jnp.einsum(
        "ai,abch->ibch",
        table_rows,
        lax.all_gather(back_modes, "gx", axis=0, tiled=True).astype(jnp.float32),
        precision=highest,
    )
    table_rows = table_y
    cell_modes = jnp.einsum(
        "bj,ibch->ijch",
        table_rows,
        lax.all_gather(over_first, "gy", axis=1, tiled=True),
        precision=highest,
    )
    spectral_cells = jnp.einsum("ck,ijch->ijkh", table_z, cell_modes, precision=highest)
    flat_grad = grad_pre.reshape(-1, channels)
    skip_part = lax.dot_general(
        flat_grad, skip_w, (((1,), (1,)), ((), ())), preferred_element_type=jnp.float32
    )
    grad_inputs = (skip_part.reshape(cells_x, cells_y, cells_z, channels) + spectral_cells).astype(
        jnp.bfloat16
    )
    local_sum = lax.dot_general(
        inputs.reshape(-1, channels),
        flat_grad,
        (((0,), (0,)), ((), ())),
        preferred_element_type=jnp.float32,
    )
    grad_skip = lax.psum(local_sum, ("gx", "gy")) / math.sqrt(length_x * length_y * cells_z)
    return (grad_inputs, grad_spectral, grad_skip)


def solution(mesh):
    in_specs = (
        P("gx", "gy", None, None),
        P("gx", "gy", None, None),
        P("gx", "gy", None, None),
        P("gx", "gy", None, None, None),
        P(),
    )
    out_specs = (P("gx", "gy", None, None), P("gx", "gy", None, None, None), P())
    return jax.shard_map(
        on_device, mesh=mesh, in_specs=in_specs, out_specs=out_specs, check_vma=False
    )
```

```python
import functools
import math

import jax
import jax.numpy as jnp
import numpy as np
from jax import lax
from jax.experimental import pallas as pl
from jax.experimental.pallas import tpu as pltpu
from jax.sharding import PartitionSpec as P

highest = lax.Precision.HIGHEST
f32 = jnp.float32
bf16 = jnp.bfloat16
LANES = 128
MIB = 1 << 20


def cas_table(modes, length, offset, cells):
    index = jnp.arange(modes, dtype=jnp.int32)
    freq = jnp.where(index < modes // 2, index, length - modes + index)
    where_cells = offset + jnp.arange(cells, dtype=jnp.int32)
    phase = freq[:, None] * where_cells[None, :] % length
    angle = phase.astype(jnp.float32) * (2.0 * math.pi / length)
    return (jnp.cos(angle) + jnp.sin(angle)) / math.sqrt(length)


def gelu_slope_of(preact_wide):
    return 0.5 * (
        1.0 + lax.erf(preact_wide * (1.0 / math.sqrt(2.0)))
    ) + preact_wide * jnp.exp(-0.5 * preact_wide * preact_wide) * (1.0 / math.sqrt(2.0 * math.pi))


def plain_cas(modes, length):
    index = np.arange(modes)
    freq = np.where(index < modes // 2, index, length - modes + index)
    angle = 2.0 * np.pi * ((freq[:, None] * np.arange(length)[None, :]) % length) / length
    return np.cos(angle) + np.sin(angle)


def rounded_table(table):
    values, counts = np.unique(np.round(np.abs(table), 12), return_counts=True)
    best = None
    for scale in np.linspace(1.0, 2.0, 512, endpoint=False):
        kept = (values * scale).astype(np.float32).astype(bf16).astype(np.float64) / scale
        error = np.sum(counts * (kept - values) ** 2)
        if best is None or error < best[0]:
            best = (error, scale)
    return (table * best[1]).astype(np.float32).astype(bf16), 1.0 / best[1]


def split_index(size, *parts):
    return np.unravel_index(np.arange(size), parts)


class Sizes:
    def __init__(self, inputs, spectral_w, gx, gy):
        self.gx, self.gy = gx, gy
        self.devices = gx * gy
        self.x, self.y, self.z, self.channels = inputs.shape
        self.cells = self.x * self.y * self.z
        self.width = 2 * self.z * self.channels // self.devices
        self.back_width = self.z * self.channels // self.devices

    def fits(self, inputs, spectral_w):
        if inputs.shape[:3] != spectral_w.shape[:3] or self.channels != LANES:
            return False
        if self.back_width * 4 != LANES or self.y % 4:
            return False
        rows = self.x * self.y // 2
        return rows == 16 and self.devices * 4 == LANES and self.x * self.y // 4 == 8 and self.z == 8


def lanes_of(shape):
    return lax.broadcasted_iota(jnp.int32, shape, len(shape) - 1)


def load(*pairs):
    copies = [pltpu.make_async_copy(source, target, sem) for source, target, sem in pairs]
    for copy in copies:
        copy.start()
    return copies


def open_kernel(s, in_hbm, pre_hbm, cot_hbm, pack_ref, grad_ref, in_ref, pre_ref, cot_ref, sems):
    copies = load(
        (in_hbm, in_ref, sems.at[0]), (pre_hbm, pre_ref, sems.at[1]), (cot_hbm, cot_ref, sems.at[2])
    )
    cells = s.cells
    place = lax.broadcasted_iota(jnp.int32, (cells, 1), 0)
    half_y = s.y // 2
    half = cells // 2
    yl, rest = place // half, place % half
    z, rest = rest // (s.x * half_y), rest % (s.x * half_y)
    x, yh = rest // half_y, rest % half_y
    source = (x * s.y + yh * 2 + yl) * s.z + z
    order = (lax.broadcasted_iota(jnp.int32, (cells, cells), 1) == source).astype(f32).astype(bf16)
    for copy in copies:
        copy.wait()
    grad = (cot_ref[...].astype(f32) * gelu_slope_of(pre_ref[...].astype(f32))).astype(bf16)
    grad_ref[...] = grad
    rows = jnp.dot(
        order, jnp.concatenate([in_ref[...], grad], 1), preferred_element_type=f32
    )
    width = LANES // 2
    low = lanes_of((half, LANES)) < width
    for field in range(2):
        even = rows[:half, field * LANES : (field + 1) * LANES]
        odd = rows[half:, field * LANES : (field + 1) * LANES]
        pack_ref[field, 0] = jnp.where(low, even, pltpu.roll(odd, width, 1)).astype(bf16)
        pack_ref[field, 1] = jnp.where(low, pltpu.roll(even, width, 1), odd).astype(bf16)


def plane_kernel(scale, x_ref, table_ref, out_ref):
    rows, width = x_ref.shape[0], LANES // 2
    made = jnp.dot(table_ref[...], x_ref[...], preferred_element_type=f32)
    low = lanes_of((rows, LANES)) < width
    straight = jnp.where(low, made[:rows], made[rows : 2 * rows])
    crossed = jnp.where(low, made[2 * rows : 3 * rows], made[3 * rows :])
    out_ref[...] = ((straight + pltpu.roll(crossed, width, 1)) * scale).astype(bf16)


def field_modes(scale, first, second, z_ref):
    width = LANES // 2
    first, second = first.astype(f32), second.astype(f32)
    low = lanes_of(first.shape) < width
    even = jnp.where(low, first, pltpu.roll(second, width, 1))
    odd = jnp.where(low, pltpu.roll(first, width, 1), second)
    rows = jnp.concatenate([even, odd], 0).astype(bf16)
    return jnp.dot(z_ref[...], rows, preferred_element_type=f32) * scale


def split_twice(value):
    high = value.astype(bf16)
    return high, (value - high.astype(f32)).astype(bf16)


def quarters(rows):
    quarter = rows.shape[0] // 4
    group_of = lanes_of((quarter, LANES)) // (LANES // 4)
    pieces = []
    for part in range(4):
        piece = rows[:quarter]
        for place in range(4):
            source = rows[place * quarter : (place + 1) * quarter]
            turn = (place - part) % 4
            moved = source if turn == 0 else pltpu.roll(source, turn * (LANES // 4), 1)
            piece = jnp.where(group_of == place, moved, piece)
        pieces.append(piece)
    return jnp.concatenate(pieces, 0)


def modes_kernel(scale, x_ref, z_ref, w_ref, field_ref, pre_ref, pack_ref, sum_ref, modes_ref, back):
    sum_ref[...] = lax.dot_general(
        field_ref[...], pre_ref[...], (((0,), (0,)), ((), ())), preferred_element_type=f32
    ).astype(bf16)
    modes_ref[...] = field_modes(scale, x_ref[1, 0], x_ref[1, 1], z_ref)
    groups = modes_ref.shape[0] // 8
    unrolled, on_vector = 16, 4
    row = lax.broadcasted_iota(jnp.int32, (8, LANES), 0)
    lane = lanes_of((LANES, LANES))

    @pl.loop(0, groups // unrolled)
    def _(turn):
        kept = jnp.zeros((LANES, LANES), f32)
        for at in range(unrolled):
            group = turn * unrolled + at
            start = pl.multiple_of(group * 8, 8)
            if at < unrolled - on_vector:
                modes = modes_ref[pl.ds(start, 8), :]
                high = modes.astype(bf16).astype(f32)
                every = lax.dot_general(
                    jnp.concatenate([high, modes - high], 0).astype(bf16),
                    w_ref[:, group].reshape(8 * LANES, LANES),
                    (((1,), (1,)), ((), ())),
                    preferred_element_type=f32,
                )
                every = every[:8] + every[8:]
                total = jnp.zeros((8, LANES), f32)
                for mode in range(8):
                    part = every[:, mode * LANES : (mode + 1) * LANES]
                    total = jnp.where(row == mode, part, total)
                back[pl.ds(start, 8), :] = total
            else:
                for mode in range(8):
                    weights = w_ref[mode, group].astype(f32)
                    total = jnp.sum(weights * modes_ref[pl.ds(start + mode, 1), :], 1, keepdims=True)
                    place = (at - unrolled + on_vector) * 8 + mode
                    kept = jnp.where(lane == place, total, kept)
        start = pl.multiple_of(((turn + 1) * unrolled - on_vector) * 8, 8)
        back[pl.ds(start, on_vector * 8), :] = kept.T[: on_vector * 8]

    rows = back[...].astype(bf16).astype(f32)
    pack_ref[...] = quarters(rows).astype(bf16)


def outer_kernel(scale, x_ref, z_ref, out_hbm, flag_ref, in_ref, grad_ref, made, sems):
    in_ref[...] = field_modes(scale, x_ref[0, 0], x_ref[0, 1], z_ref)
    grad_ref[...] = field_modes(scale, x_ref[1, 0], x_ref[1, 1], z_ref)
    flag_ref[...] = jnp.zeros(flag_ref.shape, f32)
    modes = in_ref.shape[0]
    size, unrolled = 16, 4
    row = lax.broadcasted_iota(jnp.int32, (3 * size, LANES), 0) % size

    def copy(group):
        part = pl.ds(group * size, size)
        return pltpu.make_async_copy(made.at[part], out_hbm.at[part], sems.at[group])

    @pl.loop(0, modes // size // unrolled)
    def _(turn):
        for at in range(unrolled):
            group = turn * unrolled + at
            start = pl.multiple_of(group * size, size)
            in_high, in_low = split_twice(in_ref[pl.ds(start, size), :])
            high, low = split_twice(grad_ref[pl.ds(start, size), :])
            left = jnp.concatenate([in_high, in_low, in_high], 0)
            right = jnp.concatenate([high, high, low], 0)
            zero = jnp.zeros((), bf16)
            right = jnp.concatenate([jnp.where(row == mode, right, zero) for mode in range(size)], 1)
            every = lax.dot_general(
                left, right, (((0,), (0,)), ((), ())), preferred_element_type=f32
            )
            for mode in range(size):
                made[group * size + mode] = every[:, mode * LANES : (mode + 1) * LANES].astype(bf16)
            copy(group).start()

    @pl.loop(0, modes // size)
    def _(group):
        copy(group).wait()


def back_plane_kernel(scale, x_ref, table_ref, after, out_ref):
    del after
    x = x_ref[...].astype(f32)
    rows = x.shape[0]
    turned = [x if s == 0 else pltpu.roll(x, s * (LANES // 4), 1) for s in range(4)]
    made = jnp.dot(
        table_ref[...], jnp.concatenate(turned, 0).astype(bf16), preferred_element_type=f32
    )
    group_of = lanes_of((rows, LANES)) // (LANES // 4)
    out = made[:rows]
    for place in range(1, 4):
        out = jnp.where(group_of == place, made[place * rows : (place + 1) * rows], out)
    out_ref[...] = (out * scale).astype(bf16)


def close_kernel(scale, x_ref, z_ref, pre_ref, weight_ref, sum_ref, out_ref, skip_ref):
    pieces = quarters(x_ref[...].astype(f32)).astype(bf16)
    cells = jnp.dot(z_ref[...], pieces, preferred_element_type=f32)
    part = lax.dot_general(
        pre_ref[...], weight_ref[...], (((1,), (1,)), ((), ())), preferred_element_type=f32
    )
    out_ref[...] = (part + cells * scale).astype(bf16)
    skip_ref[...] = sum_ref[...].astype(f32)


def one_hot(rows, columns):
    return (np.asarray(rows)[:, None] == np.asarray(columns)[None, :]).astype(np.float32)


def make_tables(s):
    cas_x = plain_cas(s.x * s.gx, s.x * s.gx)
    cas_y = plain_cas(s.y * s.gy, s.y * s.gy)
    cas_z = plain_cas(s.z, s.z)
    norm = math.sqrt(s.x * s.gx * s.y * s.gy)
    t = {}
    count = s.devices * s.x * s.y // 2
    px, py, x, yh = split_index(count, s.gx, s.gy, s.x, s.y // 2)
    at_x = px * s.x + x
    blocks = []
    for b, y in ((0, 0), (1, 1), (1, 0), (0, 1)):
        at_b = py * s.y + yh * 2 + b
        at_y = py * s.y + yh * 2 + y
        blocks.append(cas_x[at_x[:, None], at_x[None, :]] * cas_y[at_b[:, None], at_y[None, :]])
    t["plane"], factor = rounded_table(np.concatenate(blocks, 0))
    t["plane_scale"] = factor / norm
    a, b, c = split_index(s.cells, s.x, s.y, s.z)
    bl, z, al, bh = split_index(s.cells, 2, s.z, s.x, s.y // 2)
    same = one_hot(a * s.y + b, al * s.y + bh * 2 + bl)
    t["z"] = same * cas_z[c[:, None], z[None, :]]
    t["z_scale"] = 1.0 / math.sqrt(s.z)
    b, c, a = split_index(s.cells, s.y, s.z, s.x)
    t["z_turned"] = t["z"][(a * s.y + b) * s.z + c]
    count = s.devices * s.x
    px, py, x = split_index(count, s.gx, s.gy, s.x)
    at_x = px * s.x + x
    blocks = []
    for place in range(4):
        line = []
        for turn in range(4):
            at_y = py * s.y + place
            at_b = py * s.y + (place - turn) % 4
            line.append(cas_x[at_x[None, :], at_x[:, None]] * cas_y[at_b[None, :], at_y[:, None]])
        blocks.append(np.concatenate(line, 1))
    t["back_plane"], factor = rounded_table(np.concatenate(blocks, 0))
    t["back_plane_scale"] = factor / norm
    x, y, z = split_index(s.cells, s.x, s.y, s.z)
    yl, c, xl = split_index(s.cells, s.y, s.z, s.x)
    t["back_z"] = one_hot(x * s.y + y, xl * s.y + yl) * cas_z[c[None, :], z[:, None]]
    return {
        key: jnp.asarray(np.asarray(value, np.float32).astype(bf16))
        if isinstance(value, np.ndarray)
        else value
        for key, value in t.items()
    }


def call(kernel, out_shape, limit, flops, moved, **more):
    return pl.pallas_call(
        kernel,
        out_shape=out_shape,
        compiler_params=pltpu.CompilerParams(vmem_limit_bytes=limit * MIB),
        cost_estimate=pl.CostEstimate(flops=flops, bytes_accessed=moved, transcendentals=0),
        **more,
    )


def in_vmem(*shape, kind=bf16):
    return pltpu.VMEM(shape, kind)


def in_hbm(*shape, kind=bf16):
    return jax.ShapeDtypeStruct(shape, kind)


def exchange(pieces):
    return lax.all_to_all(pieces, ("gx", "gy"), 0, 0)


def on_device_whole_planes(s, inputs, preact, cotangent, spectral_w, skip_w):
    t = make_tables(s)
    cells, channels, devices = s.cells, s.channels, s.devices
    rows = cells // s.z // 2 * devices
    back_rows = devices * s.x
    flat = lambda array: array.reshape(cells, channels)
    vmem = pl.BlockSpec(memory_space=pltpu.VMEM)
    hbm = pl.BlockSpec(memory_space=pltpu.HBM)
    anywhere = pl.BlockSpec(memory_space=pl.ANY)
    field = pltpu.VMEM((cells, channels), bf16)
    pieces, grad_pre = call(
        functools.partial(open_kernel, s),
        (in_vmem(2, 2, cells // 2, LANES), in_vmem(cells, channels)),
        16,
        1 << 40,
        MIB,
        in_specs=[hbm] * 3,
        out_specs=(vmem, vmem),
        scratch_shapes=[field, field, field, pltpu.SemaphoreType.DMA((3,))],
    )(*(pltpu.with_memory_space_constraint(flat(a), pltpu.HBM) for a in (inputs, preact, cotangent)))
    columns = exchange(pieces.reshape(devices, -1, LANES))
    planes = call(
        functools.partial(plane_kernel, t["plane_scale"]),
        in_vmem(rows, LANES),
        16,
        1 << 36,
        4 * MIB,
        in_specs=[vmem, vmem],
        out_specs=vmem,
    )(columns.reshape(rows, LANES), t["plane"])
    owned = exchange(planes.reshape(devices, -1, LANES))
    owned = owned.reshape(2, 2, cells // 2, LANES)
    back, sums = call(
        functools.partial(modes_kernel, t["z_scale"]),
        (in_vmem(cells, channels), in_vmem(channels, channels)),
        24,
        cells * channels * channels * 16,
        9 * MIB,
        in_specs=[vmem] * 5,
        out_specs=(vmem, vmem),
        scratch_shapes=[pltpu.VMEM((cells, channels), f32), pltpu.VMEM((cells, channels), f32)],
    )(
        owned,
        t["z_turned"],
        spectral_w.reshape(s.x, s.y * s.z, channels, channels),
        flat(inputs),
        grad_pre,
    )
    pieces = lambda rows, sums: jnp.concatenate(
        [rows.reshape(devices, 4, -1), sums.reshape(devices, 4, channels)], 2
    )
    split = lambda got: (
        got[:, :, : 2 * LANES].reshape(cells, LANES),
        got[:, :, 2 * LANES :],
    )
    back_columns, sums = split(exchange(pieces(back, sums)))
    grad_spectral, flag = call(
        functools.partial(outer_kernel, t["z_scale"]),
        (in_hbm(cells, channels, channels), in_vmem(8, LANES, kind=f32)),
        24,
        cells * channels * channels * 2,
        9 * MIB,
        in_specs=[vmem] * 2,
        out_specs=(hbm, vmem),
        scratch_shapes=[
            pltpu.VMEM((cells, channels), f32),
            pltpu.VMEM((cells, channels), f32),
            pltpu.VMEM((cells, channels, channels), bf16),
            pltpu.SemaphoreType.DMA((cells // 16,)),
        ],
    )(owned, t["z"])
    skip_rows = jnp.sum(sums.astype(f32), 0) * (1.0 / math.sqrt(cells * devices))
    skip_rows = jnp.broadcast_to(skip_rows.astype(bf16), sums.shape)
    back_planes = call(
        functools.partial(back_plane_kernel, t["back_plane_scale"]),
        in_vmem(back_rows, LANES),
        16,
        back_rows * back_rows * LANES * 32,
        4 * MIB,
        in_specs=[vmem, vmem, anywhere],
        out_specs=vmem,
    )(back_columns, t["back_plane"], flag)
    spectral, sums = split(exchange(pieces(back_planes, skip_rows)))
    grad_inputs, grad_skip = call(
        functools.partial(close_kernel, t["z_scale"]),
        (in_hbm(cells, channels), in_hbm(channels, channels, kind=f32)),
        16,
        cells * cells * LANES * 4,
        MIB,
        in_specs=[vmem] * 5,
        out_specs=(vmem, vmem),
    )(spectral, t["back_z"], grad_pre, skip_w, sums.reshape(channels, channels))
    return (
        grad_inputs.reshape(inputs.shape),
        grad_spectral.reshape(spectral_w.shape),
        grad_skip,
    )


def on_device(inputs, preact, cotangent, spectral_w, skip_w):
    sizes = Sizes(inputs, spectral_w, lax.axis_size("gx"), lax.axis_size("gy"))
    if sizes.fits(inputs, spectral_w):
        return on_device_whole_planes(sizes, inputs, preact, cotangent, spectral_w, skip_w)
    return on_device_any(inputs, preact, cotangent, spectral_w, skip_w)


def on_device_any(inputs, preact, cotangent, spectral_w, skip_w):
    cells_x, cells_y, cells_z, channels = inputs.shape
    length_x = cells_x * lax.axis_size("gx")
    length_y = cells_y * lax.axis_size("gy")
    local_modes_x, local_modes_y, modes_z = (
        spectral_w.shape[0],
        spectral_w.shape[1],
        spectral_w.shape[2],
    )
    modes_x = local_modes_x * lax.axis_size("gx")
    modes_y = local_modes_y * lax.axis_size("gy")
    table_z = cas_table(modes_z, cells_z, 0, cells_z)
    table_x = cas_table(modes_x, length_x, lax.axis_index("gx") * cells_x, cells_x)
    table_y = cas_table(modes_y, length_y, lax.axis_index("gy") * cells_y, cells_y)
    preact_wide = preact.astype(jnp.float32)
    gelu_slope = 0.5 * (
        1.0 + lax.erf(preact_wide * (1.0 / math.sqrt(2.0)))
    ) + preact_wide * jnp.exp(-0.5 * preact_wide * preact_wide) * (1.0 / math.sqrt(2.0 * math.pi))
    grad_pre = (cotangent.astype(jnp.float32) * gelu_slope).astype(jnp.bfloat16)
    fields = jnp.stack([inputs, grad_pre]).astype(jnp.float32)
    z_modes = jnp.einsum("ck,fijkh->fijch", table_z, fields, precision=highest)
    table_rows = table_y
    part_y = lax.psum_scatter(
        jnp.einsum("bj,fijch->bfich", table_rows, z_modes, precision=highest),
        "gy",
        scatter_dimension=0,
        tiled=True,
    )
    table_rows = table_x
    owned_modes = lax.psum_scatter(
        jnp.einsum("ai,bfich->abfch", table_rows, part_y, precision=highest),
        "gx",
        scatter_dimension=0,
        tiled=True,
    )
    input_modes = owned_modes[:, :, 0]
    grad_modes = owned_modes[:, :, 1]
    grad_spectral = jnp.einsum(
        "abcp,abcq->abcpq", input_modes, grad_modes, precision=highest
    ).astype(jnp.bfloat16)
    back_modes = jnp.einsum(
        "abcq,abcpq->abcp", grad_modes, spectral_w.astype(jnp.float32), precision=highest
    ).astype(jnp.bfloat16)
    table_rows = table_x
    over_first = jnp.einsum(
        "ai,abch->ibch",
        table_rows,
        lax.all_gather(back_modes, "gx", axis=0, tiled=True).astype(jnp.float32),
        precision=highest,
    )
    table_rows = table_y
    cell_modes = jnp.einsum(
        "bj,ibch->ijch",
        table_rows,
        lax.all_gather(over_first, "gy", axis=1, tiled=True),
        precision=highest,
    )
    spectral_cells = jnp.einsum("ck,ijch->ijkh", table_z, cell_modes, precision=highest)
    flat_grad = grad_pre.reshape(-1, channels)
    skip_part = lax.dot_general(
        flat_grad, skip_w, (((1,), (1,)), ((), ())), preferred_element_type=jnp.float32
    )
    grad_inputs = (skip_part.reshape(cells_x, cells_y, cells_z, channels) + spectral_cells).astype(
        jnp.bfloat16
    )
    local_sum = lax.dot_general(
        inputs.reshape(-1, channels),
        flat_grad,
        (((0,), (0,)), ((), ())),
        preferred_element_type=jnp.float32,
    )
    grad_skip = lax.psum(local_sum, ("gx", "gy")) / math.sqrt(length_x * length_y * cells_z)
    return (grad_inputs, grad_spectral, grad_skip)


def solution(mesh):
    in_specs = (
        P("gx", "gy", None, None),
        P("gx", "gy", None, None),
        P("gx", "gy", None, None),
        P("gx", "gy", None, None, None),
        P(),
    )
    out_specs = (P("gx", "gy", None, None), P("gx", "gy", None, None, None), P())
    return jax.shard_map(
        on_device, mesh=mesh, in_specs=in_specs, out_specs=out_specs, check_vma=False
    )
```

```python
import functools
import math

import jax
import jax.numpy as jnp
import numpy as np
from jax import lax
from jax.experimental import pallas as pl
from jax.experimental.pallas import tpu as pltpu
from jax.sharding import PartitionSpec as P

highest = lax.Precision.HIGHEST
f32 = jnp.float32
bf16 = jnp.bfloat16
LANES = 128
MIB = 1 << 20


def cas_table(modes, length, offset, cells):
    index = jnp.arange(modes, dtype=jnp.int32)
    freq = jnp.where(index < modes // 2, index, length - modes + index)
    where_cells = offset + jnp.arange(cells, dtype=jnp.int32)
    phase = freq[:, None] * where_cells[None, :] % length
    angle = phase.astype(jnp.float32) * (2.0 * math.pi / length)
    return (jnp.cos(angle) + jnp.sin(angle)) / math.sqrt(length)


def gelu_slope_of(preact_wide):
    return 0.5 * (
        1.0 + lax.erf(preact_wide * (1.0 / math.sqrt(2.0)))
    ) + preact_wide * jnp.exp(-0.5 * preact_wide * preact_wide) * (1.0 / math.sqrt(2.0 * math.pi))


def plain_cas(modes, length):
    index = np.arange(modes)
    freq = np.where(index < modes // 2, index, length - modes + index)
    angle = 2.0 * np.pi * ((freq[:, None] * np.arange(length)[None, :]) % length) / length
    return np.cos(angle) + np.sin(angle)


def rounded_table(table):
    values, counts = np.unique(np.round(np.abs(table), 12), return_counts=True)
    best = None
    for scale in np.linspace(1.0, 2.0, 512, endpoint=False):
        kept = (values * scale).astype(np.float32).astype(bf16).astype(np.float64) / scale
        error = np.sum(counts * (kept - values) ** 2)
        if best is None or error < best[0]:
            best = (error, scale)
    return (table * best[1]).astype(np.float32).astype(bf16), 1.0 / best[1]


def split_index(size, *parts):
    return np.unravel_index(np.arange(size), parts)


class Sizes:
    def __init__(self, inputs, spectral_w, gx, gy):
        self.gx, self.gy = gx, gy
        self.devices = gx * gy
        self.x, self.y, self.z, self.channels = inputs.shape
        self.cells = self.x * self.y * self.z
        self.width = 2 * self.z * self.channels // self.devices
        self.back_width = self.z * self.channels // self.devices

    def fits(self, inputs, spectral_w):
        if inputs.shape[:3] != spectral_w.shape[:3] or self.channels != LANES:
            return False
        if self.back_width * 4 != LANES or self.y % 4:
            return False
        rows = self.x * self.y // 2
        return rows == 16 and self.devices * 4 == LANES and self.x * self.y // 4 == 8 and self.z == 8


def lanes_of(shape):
    return lax.broadcasted_iota(jnp.int32, shape, len(shape) - 1)


def load(*pairs):
    copies = [pltpu.make_async_copy(source, target, sem) for source, target, sem in pairs]
    for copy in copies:
        copy.start()
    return copies


def open_kernel(s, in_hbm, pre_hbm, cot_hbm, pack_ref, grad_ref, in_ref, pre_ref, cot_ref, sems):
    copies = load(
        (in_hbm, in_ref, sems.at[0]), (pre_hbm, pre_ref, sems.at[1]), (cot_hbm, cot_ref, sems.at[2])
    )
    cells = s.cells
    place = lax.broadcasted_iota(jnp.int32, (cells, 1), 0)
    half_y = s.y // 2
    half = cells // 2
    yl, rest = place // half, place % half
    z, rest = rest // (s.x * half_y), rest % (s.x * half_y)
    yh, x = rest // s.x, rest % s.x
    source = (x * s.y + yh * 2 + yl) * s.z + z
    order = (lax.broadcasted_iota(jnp.int32, (cells, cells), 1) == source).astype(f32).astype(bf16)
    for copy in copies:
        copy.wait()
    grad = (cot_ref[...].astype(f32) * gelu_slope_of(pre_ref[...].astype(f32))).astype(bf16)
    grad_ref[...] = grad
    rows = jnp.dot(
        order, jnp.concatenate([in_ref[...], grad], 1), preferred_element_type=f32
    )
    width = LANES // 2
    low = lanes_of((half, LANES)) < width
    for field in range(2):
        even = rows[:half, field * LANES : (field + 1) * LANES]
        odd = rows[half:, field * LANES : (field + 1) * LANES]
        pack_ref[field, 0] = jnp.where(low, even, pltpu.roll(odd, width, 1)).astype(bf16)
        pack_ref[field, 1] = jnp.where(low, pltpu.roll(even, width, 1), odd).astype(bf16)


def first_axis(tiles, table_ref, along, across):
    lines = [tiles[:, j].reshape(along * 8, LANES) for j in range(across)]
    lines = jnp.concatenate(lines, 1).astype(bf16)
    made = jnp.dot(
        table_ref[...], jnp.concatenate([lines, lines], 0), preferred_element_type=f32
    )
    return [
        jnp.concatenate(
            [made[i * 8 : i * 8 + 8, j * LANES : (j + 1) * LANES] for j in range(across)], 0
        )
        for i in range(along)
    ]


def plane_kernel(s, scale, x_ref, first_ref, second_ref, out_ref):
    width = LANES // 2
    across = s.gy * s.y // 2
    tiles = x_ref[...].astype(f32).reshape(s.gx, across, 8, LANES)
    parts = jnp.concatenate(first_axis(tiles, first_ref, s.gx, across), 1)
    rows = across * 8
    table = second_ref[...]
    made = jnp.dot(
        jnp.concatenate([table, table], 1),
        jnp.concatenate(split_twice(parts), 0),
        preferred_element_type=f32,
    )
    low = lanes_of((rows, LANES)) < width
    for part in range(s.gx):
        here = made[:, part * LANES : (part + 1) * LANES]
        straight = jnp.where(low, here[:rows], here[rows : 2 * rows])
        crossed = jnp.where(low, here[2 * rows : 3 * rows], here[3 * rows :])
        value = (straight + pltpu.roll(crossed, width, 1)) * scale
        out_ref[part * rows : (part + 1) * rows, :] = value.astype(bf16)


def field_modes(scale, first, second, z_ref):
    width = LANES // 2
    first, second = first.astype(f32), second.astype(f32)
    low = lanes_of(first.shape) < width
    even = jnp.where(low, first, pltpu.roll(second, width, 1))
    odd = jnp.where(low, pltpu.roll(first, width, 1), second)
    rows = jnp.concatenate([even, odd], 0).astype(bf16)
    return jnp.dot(z_ref[...], rows, preferred_element_type=f32) * scale


def split_twice(value):
    high = value.astype(bf16)
    return high, (value - high.astype(f32)).astype(bf16)


def quarters(rows):
    quarter = rows.shape[0] // 4
    group_of = lanes_of((quarter, LANES)) // (LANES // 4)
    pieces = []
    for part in range(4):
        piece = rows[:quarter]
        for place in range(4):
            source = rows[place * quarter : (place + 1) * quarter]
            turn = (place - part) % 4
            moved = source if turn == 0 else pltpu.roll(source, turn * (LANES // 4), 1)
            piece = jnp.where(group_of == place, moved, piece)
        pieces.append(piece)
    return jnp.concatenate(pieces, 0)


def modes_kernel(scale, x_ref, z_ref, w_ref, field_ref, pre_ref, pack_ref, sum_ref, modes_ref, back):
    sum_ref[...] = lax.dot_general(
        field_ref[...], pre_ref[...], (((0,), (0,)), ((), ())), preferred_element_type=f32
    ).astype(bf16)
    modes_ref[...] = field_modes(scale, x_ref[1, 0], x_ref[1, 1], z_ref)
    groups = modes_ref.shape[0] // 8
    unrolled, on_vector = 16, 4
    row = lax.broadcasted_iota(jnp.int32, (8, LANES), 0)
    lane = lanes_of((LANES, LANES))

    @pl.loop(0, groups // unrolled)
    def _(turn):
        kept = jnp.zeros((LANES, LANES), f32)
        for at in range(unrolled):
            group = turn * unrolled + at
            start = pl.multiple_of(group * 8, 8)
            if at < unrolled - on_vector:
                modes = modes_ref[pl.ds(start, 8), :]
                high = modes.astype(bf16).astype(f32)
                every = lax.dot_general(
                    jnp.concatenate([high, modes - high], 0).astype(bf16),
                    w_ref[:, group].reshape(8 * LANES, LANES),
                    (((1,), (1,)), ((), ())),
                    preferred_element_type=f32,
                )
                every = every[:8] + every[8:]
                total = jnp.zeros((8, LANES), f32)
                for mode in range(8):
                    part = every[:, mode * LANES : (mode + 1) * LANES]
                    total = jnp.where(row == mode, part, total)
                back[pl.ds(start, 8), :] = total
            else:
                for mode in range(8):
                    weights = w_ref[mode, group].astype(f32)
                    total = jnp.sum(weights * modes_ref[pl.ds(start + mode, 1), :], 1, keepdims=True)
                    place = (at - unrolled + on_vector) * 8 + mode
                    kept = jnp.where(lane == place, total, kept)
        start = pl.multiple_of(((turn + 1) * unrolled - on_vector) * 8, 8)
        back[pl.ds(start, on_vector * 8), :] = kept.T[: on_vector * 8]

    rows = back[...].astype(bf16).astype(f32)
    pack_ref[...] = quarters(rows).astype(bf16)


def outer_kernel(scale, x_ref, z_ref, grad_ref, after, out_hbm, in_ref, made, sems):
    in_ref[...] = field_modes(scale, x_ref[0, 0], x_ref[0, 1], z_ref)
    del after
    lines, columns = made.shape[:2]
    across = 2
    size, unrolled = across * lines, 4
    groups = columns // across
    row = lax.broadcasted_iota(jnp.int32, (3 * size, LANES), 0) % size

    def copy(group):
        part = pl.ds(group * across, across)
        return pltpu.make_async_copy(made.at[:, part], out_hbm.at[:, part], sems.at[group])

    @pl.loop(0, groups // unrolled)
    def _(turn):
        for at in range(unrolled):
            group = turn * unrolled + at
            start = pl.multiple_of(group * size, size)
            in_high, in_low = split_twice(in_ref[pl.ds(start, size), :])
            high, low = split_twice(grad_ref[pl.ds(start, size), :])
            left = jnp.concatenate([in_high, in_low, in_high], 0)
            right = jnp.concatenate([high, high, low], 0)
            zero = jnp.zeros((), bf16)
            right = jnp.concatenate([jnp.where(row == mode, right, zero) for mode in range(size)], 1)
            every = lax.dot_general(
                left, right, (((0,), (0,)), ((), ())), preferred_element_type=f32
            )
            for mode in range(size):
                part = every[:, mode * LANES : (mode + 1) * LANES].astype(bf16)
                made[mode % lines, group * across + mode // lines] = part
            copy(group).start()

    @pl.loop(0, groups)
    def _(group):
        copy(group).wait()


def back_plane_kernel(s, scale, x_ref, first_ref, second_ref, out_ref):
    tiles = x_ref[...].astype(f32).reshape(s.gx, s.gy, 8, LANES)
    parts = jnp.concatenate(first_axis(tiles, first_ref, s.gx, s.gy), 1)
    rows, across = parts.shape
    wide = across // LANES
    turned = [parts]
    for turn in range(1, 4):
        moved = [
            pltpu.roll(parts[:, i * LANES : (i + 1) * LANES], turn * (LANES // 4), 1)
            for i in range(wide)
        ]
        turned.append(jnp.concatenate(moved, 1))
    high, low = split_twice(jnp.concatenate(turned, 0))
    table = second_ref[...]
    made = jnp.dot(
        jnp.concatenate([table, table], 1),
        jnp.concatenate([high, low], 0),
        preferred_element_type=f32,
    )
    group_of = lanes_of((rows, LANES)) // (LANES // 4)
    for part in range(wide):
        here = made[:, part * LANES : (part + 1) * LANES]
        value = here[:rows]
        for place in range(1, 4):
            value = jnp.where(group_of == place, here[place * rows : (place + 1) * rows], value)
        out_ref[part * rows : (part + 1) * rows, :] = (value * scale).astype(bf16)


def close_kernel(scale, x_ref, z_ref, pre_ref, weight_ref, sum_ref, out_ref, skip_ref):
    pieces = quarters(x_ref[...].astype(f32)).astype(bf16)
    cells = jnp.dot(z_ref[...], pieces, preferred_element_type=f32)
    part = lax.dot_general(
        pre_ref[...], weight_ref[...], (((1,), (1,)), ((), ())), preferred_element_type=f32
    )
    out_ref[...] = (part + cells * scale).astype(bf16)
    skip_ref[...] = sum_ref[...].astype(f32)


def one_hot(rows, columns):
    return (np.asarray(rows)[:, None] == np.asarray(columns)[None, :]).astype(np.float32)


def twice(table):
    high = table.astype(np.float32).astype(bf16)
    low = (table - high.astype(np.float64)).astype(np.float32).astype(bf16)
    return np.concatenate([high, low], 1)


def make_tables(s):
    cas_x = plain_cas(s.x * s.gx, s.x * s.gx)
    cas_y = plain_cas(s.y * s.gy, s.y * s.gy)
    cas_z = plain_cas(s.z, s.z)
    norm = math.sqrt(s.x * s.gx * s.y * s.gy)
    t = {}
    t["first"] = twice(cas_x)
    t["back_first"] = twice(cas_x.T)
    count = s.gy * s.y // 2 * s.x
    py, yh, x = split_index(count, s.gy, s.y // 2, s.x)
    at = py * s.y + yh * 2
    same = one_hot(x, x)
    blocks = [cas_y[(at + b)[:, None], (at + y)[None, :]] * same for b, y in ((0, 0), (1, 1), (1, 0), (0, 1))]
    t["second"], factor = rounded_table(np.concatenate(blocks, 0))
    t["scale"] = factor / norm
    b, c, a = split_index(s.cells, s.y, s.z, s.x)
    bl, z, bh, al = split_index(s.cells, 2, s.z, s.y // 2, s.x)
    same = one_hot(a * s.y + b, al * s.y + bh * 2 + bl)
    t["z"] = same * cas_z[c[:, None], z[None, :]]
    t["z_scale"] = 1.0 / math.sqrt(s.z)
    py, x = split_index(s.gy * s.x, s.gy, s.x)
    same = one_hot(x, x)
    blocks = []
    for place in range(4):
        line = []
        for turn in range(4):
            at_y = py * s.y + place
            at_b = py * s.y + (place - turn) % 4
            line.append(cas_y[at_b[None, :], at_y[:, None]] * same)
        blocks.append(np.concatenate(line, 1))
    t["back_second"], factor = rounded_table(np.concatenate(blocks, 0))
    t["back_scale"] = factor / norm
    x, y, z = split_index(s.cells, s.x, s.y, s.z)
    yl, c, xl = split_index(s.cells, s.y, s.z, s.x)
    t["back_z"] = one_hot(x * s.y + y, xl * s.y + yl) * cas_z[c[None, :], z[:, None]]
    return {
        key: jnp.asarray(np.asarray(value, np.float32).astype(bf16))
        if isinstance(value, np.ndarray)
        else value
        for key, value in t.items()
    }


def call(kernel, out_shape, limit, flops, moved, **more):
    return pl.pallas_call(
        kernel,
        out_shape=out_shape,
        compiler_params=pltpu.CompilerParams(vmem_limit_bytes=limit * MIB),
        cost_estimate=pl.CostEstimate(flops=flops, bytes_accessed=moved, transcendentals=0),
        **more,
    )


def in_vmem(*shape, kind=bf16):
    return pltpu.VMEM(shape, kind)


def in_hbm(*shape, kind=bf16):
    return jax.ShapeDtypeStruct(shape, kind)


def exchange(pieces):
    return lax.all_to_all(pieces, ("gx", "gy"), 0, 0)


def on_device_whole_planes(s, inputs, preact, cotangent, spectral_w, skip_w):
    t = make_tables(s)
    cells, channels, devices = s.cells, s.channels, s.devices
    rows = cells // s.z // 2 * devices
    back_rows = devices * s.x
    flat = lambda array: array.reshape(cells, channels)
    vmem = pl.BlockSpec(memory_space=pltpu.VMEM)
    hbm = pl.BlockSpec(memory_space=pltpu.HBM)
    anywhere = pl.BlockSpec(memory_space=pl.ANY)
    field = pltpu.VMEM((cells, channels), bf16)
    pieces, grad_pre = call(
        functools.partial(open_kernel, s),
        (in_vmem(2, 2, cells // 2, LANES), in_vmem(cells, channels)),
        16,
        1 << 40,
        MIB,
        in_specs=[hbm] * 3,
        out_specs=(vmem, vmem),
        scratch_shapes=[field, field, field, pltpu.SemaphoreType.DMA((3,))],
    )(*(pltpu.with_memory_space_constraint(flat(a), pltpu.HBM) for a in (inputs, preact, cotangent)))
    columns = exchange(pieces.reshape(devices, -1, LANES))
    planes = call(
        functools.partial(plane_kernel, s, t["scale"]),
        in_vmem(rows, LANES),
        16,
        1 << 36,
        MIB,
        in_specs=[vmem] * 3,
        out_specs=vmem,
    )(columns.reshape(rows, LANES), t["first"], t["second"])
    owned = exchange(planes.reshape(devices, -1, LANES))
    owned = owned.reshape(2, 2, cells // 2, LANES)
    back, sums, grad_modes = call(
        functools.partial(modes_kernel, t["z_scale"]),
        (
            in_vmem(cells, channels),
            in_vmem(channels, channels),
            in_vmem(cells, channels, kind=f32),
        ),
        24,
        cells * channels * channels * 16,
        9 * MIB,
        in_specs=[vmem] * 5,
        out_specs=(vmem, vmem, vmem),
        scratch_shapes=[pltpu.VMEM((cells, channels), f32)],
    )(
        owned,
        t["z"],
        spectral_w.reshape(s.x, s.y * s.z, channels, channels),
        flat(inputs),
        grad_pre,
    )
    pieces = lambda rows, sums: jnp.concatenate(
        [rows.reshape(devices, 4, -1), sums.reshape(devices, 4, channels)], 2
    )
    split = lambda got: (
        got[:, :, : 2 * LANES].reshape(cells, LANES),
        got[:, :, 2 * LANES :],
    )
    back_columns, sums = split(exchange(pieces(back, sums)))
    skip_rows = jnp.sum(sums.astype(f32), 0) * (1.0 / math.sqrt(cells * devices))
    skip_rows = jnp.broadcast_to(skip_rows.astype(bf16), sums.shape)
    back_planes = call(
        functools.partial(back_plane_kernel, s, t["back_scale"]),
        in_vmem(back_rows, LANES),
        16,
        back_rows * back_rows * LANES * 8,
        MIB,
        in_specs=[vmem] * 3,
        out_specs=vmem,
    )(back_columns, t["back_first"], t["back_second"])
    split_modes = (s.x, s.y * s.z, channels, channels)
    grad_spectral = call(
        functools.partial(outer_kernel, t["z_scale"]),
        in_hbm(*split_modes),
        24,
        cells * channels * channels * 2,
        9 * MIB,
        in_specs=[vmem] * 3 + [anywhere],
        out_specs=hbm,
        scratch_shapes=[
            pltpu.VMEM((cells, channels), f32),
            pltpu.VMEM(split_modes, bf16),
            pltpu.SemaphoreType.DMA((s.y * s.z // 2,)),
        ],
    )(owned, t["z"], grad_modes, back_planes)
    spectral, sums = split(exchange(pieces(back_planes, skip_rows)))
    grad_inputs, grad_skip = call(
        functools.partial(close_kernel, t["z_scale"]),
        (in_hbm(cells, channels), in_hbm(channels, channels, kind=f32)),
        16,
        cells * cells * LANES * 4,
        MIB,
        in_specs=[vmem] * 5,
        out_specs=(vmem, vmem),
    )(spectral, t["back_z"], grad_pre, skip_w, sums.reshape(channels, channels))
    return (
        grad_inputs.reshape(inputs.shape),
        grad_spectral.reshape(spectral_w.shape),
        grad_skip,
    )


def on_device(inputs, preact, cotangent, spectral_w, skip_w):
    sizes = Sizes(inputs, spectral_w, lax.axis_size("gx"), lax.axis_size("gy"))
    if sizes.fits(inputs, spectral_w):
        return on_device_whole_planes(sizes, inputs, preact, cotangent, spectral_w, skip_w)
    return on_device_any(inputs, preact, cotangent, spectral_w, skip_w)


def on_device_any(inputs, preact, cotangent, spectral_w, skip_w):
    cells_x, cells_y, cells_z, channels = inputs.shape
    length_x = cells_x * lax.axis_size("gx")
    length_y = cells_y * lax.axis_size("gy")
    local_modes_x, local_modes_y, modes_z = (
        spectral_w.shape[0],
        spectral_w.shape[1],
        spectral_w.shape[2],
    )
    modes_x = local_modes_x * lax.axis_size("gx")
    modes_y = local_modes_y * lax.axis_size("gy")
    table_z = cas_table(modes_z, cells_z, 0, cells_z)
    table_x = cas_table(modes_x, length_x, lax.axis_index("gx") * cells_x, cells_x)
    table_y = cas_table(modes_y, length_y, lax.axis_index("gy") * cells_y, cells_y)
    preact_wide = preact.astype(jnp.float32)
    gelu_slope = 0.5 * (
        1.0 + lax.erf(preact_wide * (1.0 / math.sqrt(2.0)))
    ) + preact_wide * jnp.exp(-0.5 * preact_wide * preact_wide) * (1.0 / math.sqrt(2.0 * math.pi))
    grad_pre = (cotangent.astype(jnp.float32) * gelu_slope).astype(jnp.bfloat16)
    fields = jnp.stack([inputs, grad_pre]).astype(jnp.float32)
    z_modes = jnp.einsum("ck,fijkh->fijch", table_z, fields, precision=highest)
    table_rows = table_y
    part_y = lax.psum_scatter(
        jnp.einsum("bj,fijch->bfich", table_rows, z_modes, precision=highest),
        "gy",
        scatter_dimension=0,
        tiled=True,
    )
    table_rows = table_x
    owned_modes = lax.psum_scatter(
        jnp.einsum("ai,bfich->abfch", table_rows, part_y, precision=highest),
        "gx",
        scatter_dimension=0,
        tiled=True,
    )
    input_modes = owned_modes[:, :, 0]
    grad_modes = owned_modes[:, :, 1]
    grad_spectral = jnp.einsum(
        "abcp,abcq->abcpq", input_modes, grad_modes, precision=highest
    ).astype(jnp.bfloat16)
    back_modes = jnp.einsum(
        "abcq,abcpq->abcp", grad_modes, spectral_w.astype(jnp.float32), precision=highest
    ).astype(jnp.bfloat16)
    table_rows = table_x
    over_first = jnp.einsum(
        "ai,abch->ibch",
        table_rows,
        lax.all_gather(back_modes, "gx", axis=0, tiled=True).astype(jnp.float32),
        precision=highest,
    )
    table_rows = table_y
    cell_modes = jnp.einsum(
        "bj,ibch->ijch",
        table_rows,
        lax.all_gather(over_first, "gy", axis=1, tiled=True),
        precision=highest,
    )
    spectral_cells = jnp.einsum("ck,ijch->ijkh", table_z, cell_modes, precision=highest)
    flat_grad = grad_pre.reshape(-1, channels)
    skip_part = lax.dot_general(
        flat_grad, skip_w, (((1,), (1,)), ((), ())), preferred_element_type=jnp.float32
    )
    grad_inputs = (skip_part.reshape(cells_x, cells_y, cells_z, channels) + spectral_cells).astype(
        jnp.bfloat16
    )
    local_sum = lax.dot_general(
        inputs.reshape(-1, channels),
        flat_grad,
        (((0,), (0,)), ((), ())),
        preferred_element_type=jnp.float32,
    )
    grad_skip = lax.psum(local_sum, ("gx", "gy")) / math.sqrt(length_x * length_y * cells_z)
    return (grad_inputs, grad_spectral, grad_skip)


def solution(mesh):
    in_specs = (
        P("gx", "gy", None, None),
        P("gx", "gy", None, None),
        P("gx", "gy", None, None),
        P("gx", "gy", None, None, None),
        P(),
    )
    out_specs = (P("gx", "gy", None, None), P("gx", "gy", None, None, None), P())
    return jax.shard_map(
        on_device, mesh=mesh, in_specs=in_specs, out_specs=out_specs, check_vma=False
    )
```

```python
import functools
import math

import jax
import jax.numpy as jnp
import numpy as np
from jax import lax
from jax.experimental import pallas as pl
from jax.experimental.pallas import tpu as pltpu
from jax.sharding import PartitionSpec as P

highest = lax.Precision.HIGHEST
f32 = jnp.float32
bf16 = jnp.bfloat16
LANES = 128
MIB = 1 << 20


def cas_table(modes, length, offset, cells):
    index = jnp.arange(modes, dtype=jnp.int32)
    freq = jnp.where(index < modes // 2, index, length - modes + index)
    where_cells = offset + jnp.arange(cells, dtype=jnp.int32)
    phase = freq[:, None] * where_cells[None, :] % length
    angle = phase.astype(jnp.float32) * (2.0 * math.pi / length)
    return (jnp.cos(angle) + jnp.sin(angle)) / math.sqrt(length)


def gelu_slope_of(preact_wide):
    return 0.5 * (
        1.0 + lax.erf(preact_wide * (1.0 / math.sqrt(2.0)))
    ) + preact_wide * jnp.exp(-0.5 * preact_wide * preact_wide) * (1.0 / math.sqrt(2.0 * math.pi))


def plain_cas(modes, length):
    index = np.arange(modes)
    freq = np.where(index < modes // 2, index, length - modes + index)
    angle = 2.0 * np.pi * ((freq[:, None] * np.arange(length)[None, :]) % length) / length
    return np.cos(angle) + np.sin(angle)


def rounded_table(table):
    values, counts = np.unique(np.round(np.abs(table), 12), return_counts=True)
    best = None
    for scale in np.linspace(1.0, 2.0, 512, endpoint=False):
        kept = (values * scale).astype(np.float32).astype(bf16).astype(np.float64) / scale
        error = np.sum(counts * (kept - values) ** 2)
        if best is None or error < best[0]:
            best = (error, scale)
    return (table * best[1]).astype(np.float32).astype(bf16), 1.0 / best[1]


def split_index(size, *parts):
    return np.unravel_index(np.arange(size), parts)


class Sizes:
    def __init__(self, inputs, spectral_w, gx, gy):
        self.gx, self.gy = gx, gy
        self.devices = gx * gy
        self.x, self.y, self.z, self.channels = inputs.shape
        self.cells = self.x * self.y * self.z
        self.width = 2 * self.z * self.channels // self.devices
        self.back_width = self.z * self.channels // self.devices

    def fits(self, inputs, spectral_w):
        if inputs.shape[:3] != spectral_w.shape[:3] or self.channels != LANES:
            return False
        if self.back_width * 4 != LANES or self.y % 4:
            return False
        rows = self.x * self.y // 2
        return rows == 16 and self.devices * 4 == LANES and self.x * self.y // 4 == 8 and self.z == 8


def lanes_of(shape):
    return lax.broadcasted_iota(jnp.int32, shape, len(shape) - 1)


def load(*pairs):
    copies = [pltpu.make_async_copy(source, target, sem) for source, target, sem in pairs]
    for copy in copies:
        copy.start()
    return copies


def open_kernel(s, in_hbm, pre_hbm, cot_hbm, pack_ref, grad_ref, in_ref, pre_ref, cot_ref, sems):
    copies = load(
        (in_hbm, in_ref, sems.at[0]), (pre_hbm, pre_ref, sems.at[1]), (cot_hbm, cot_ref, sems.at[2])
    )
    cells = s.cells
    place = lax.broadcasted_iota(jnp.int32, (cells, 1), 0)
    half_y = s.y // 2
    half = cells // 2
    yl, rest = place // half, place % half
    z, rest = rest // (s.x * half_y), rest % (s.x * half_y)
    yh, x = rest // s.x, rest % s.x
    source = (x * s.y + yh * 2 + yl) * s.z + z
    order = (lax.broadcasted_iota(jnp.int32, (cells, cells), 1) == source).astype(f32).astype(bf16)
    for copy in copies:
        copy.wait()
    grad = (cot_ref[...].astype(f32) * gelu_slope_of(pre_ref[...].astype(f32))).astype(bf16)
    grad_ref[...] = grad
    rows = jnp.dot(
        order, jnp.concatenate([in_ref[...], grad], 1), preferred_element_type=f32
    )
    width = LANES // 2
    low = lanes_of((half, LANES)) < width
    for field in range(2):
        even = rows[:half, field * LANES : (field + 1) * LANES]
        odd = rows[half:, field * LANES : (field + 1) * LANES]
        pack_ref[field, 0] = jnp.where(low, even, pltpu.roll(odd, width, 1)).astype(bf16)
        pack_ref[field, 1] = jnp.where(low, pltpu.roll(even, width, 1), odd).astype(bf16)


def first_axis(tiles, table_ref, along, across):
    lines = [tiles[:, j].reshape(along * 8, LANES) for j in range(across)]
    lines = jnp.concatenate(lines, 1).astype(bf16)
    made = jnp.dot(
        table_ref[...], jnp.concatenate([lines, lines], 0), preferred_element_type=f32
    )
    return [
        jnp.concatenate(
            [made[i * 8 : i * 8 + 8, j * LANES : (j + 1) * LANES] for j in range(across)], 0
        )
        for i in range(along)
    ]


def plane_kernel(s, scale, x_ref, first_ref, second_ref, out_ref):
    width = LANES // 2
    across = s.gy * s.y // 2
    tiles = x_ref[...].astype(f32).reshape(s.gx, across, 8, LANES)
    parts = jnp.concatenate(first_axis(tiles, first_ref, s.gx, across), 1)
    rows = across * 8
    table = second_ref[...]
    made = jnp.dot(
        jnp.concatenate([table, table], 1),
        jnp.concatenate(split_twice(parts), 0),
        preferred_element_type=f32,
    )
    low = lanes_of((rows, LANES)) < width
    for part in range(s.gx):
        here = made[:, part * LANES : (part + 1) * LANES]
        straight = jnp.where(low, here[:rows], here[rows : 2 * rows])
        crossed = jnp.where(low, here[2 * rows : 3 * rows], here[3 * rows :])
        value = (straight + pltpu.roll(crossed, width, 1)) * scale
        out_ref[part * rows : (part + 1) * rows, :] = value.astype(bf16)


def field_modes(scale, first, second, z_ref):
    width = LANES // 2
    first, second = first.astype(f32), second.astype(f32)
    low = lanes_of(first.shape) < width
    even = jnp.where(low, first, pltpu.roll(second, width, 1))
    odd = jnp.where(low, pltpu.roll(first, width, 1), second)
    rows = jnp.concatenate([even, odd], 0).astype(bf16)
    return jnp.dot(z_ref[...], rows, preferred_element_type=f32) * scale


def split_twice(value):
    high = value.astype(bf16)
    return high, (value - high.astype(f32)).astype(bf16)


def quarters(rows):
    quarter = rows.shape[0] // 4
    group_of = lanes_of((quarter, LANES)) // (LANES // 4)
    pieces = []
    for part in range(4):
        piece = rows[:quarter]
        for place in range(4):
            source = rows[place * quarter : (place + 1) * quarter]
            turn = (place - part) % 4
            moved = source if turn == 0 else pltpu.roll(source, turn * (LANES // 4), 1)
            piece = jnp.where(group_of == place, moved, piece)
        pieces.append(piece)
    return jnp.concatenate(pieces, 0)


def modes_kernel(scale, x_ref, z_ref, w_ref, field_ref, pre_ref, pack_ref, sum_ref, modes_ref, back):
    sum_ref[...] = lax.dot_general(
        field_ref[...], pre_ref[...], (((0,), (0,)), ((), ())), preferred_element_type=f32
    ).astype(bf16)
    modes_ref[...] = field_modes(scale, x_ref[1, 0], x_ref[1, 1], z_ref)
    groups = modes_ref.shape[0] // 8
    row = lax.broadcasted_iota(jnp.int32, (8, LANES), 0)
    lane = lanes_of((LANES, LANES))
    on_vector = [group for group in range(groups) if group * 10 // groups != (group + 1) * 10 // groups]
    kept = jnp.zeros((LANES, LANES), f32)
    for group in range(groups):
        start = group * 8
        if group in on_vector:
            for mode in range(8):
                weights = w_ref[mode, group].astype(f32)
                total = jnp.sum(weights * modes_ref[start + mode : start + mode + 1, :], 1, keepdims=True)
                kept = jnp.where(lane == on_vector.index(group) * 8 + mode, total, kept)
            continue
        modes = modes_ref[start : start + 8, :]
        high = modes.astype(bf16).astype(f32)
        every = lax.dot_general(
            jnp.concatenate([high, modes - high], 0).astype(bf16),
            w_ref[:, group].reshape(8 * LANES, LANES),
            (((1,), (1,)), ((), ())),
            preferred_element_type=f32,
        )
        every = every[:8] + every[8:]
        total = jnp.zeros((8, LANES), f32)
        for mode in range(8):
            total = jnp.where(row == mode, every[:, mode * LANES : (mode + 1) * LANES], total)
        back[start : start + 8, :] = total
    kept = kept.T
    for at, group in enumerate(on_vector):
        back[group * 8 : group * 8 + 8, :] = kept[at * 8 : at * 8 + 8]

    rows = back[...].astype(bf16).astype(f32)
    pack_ref[...] = quarters(rows).astype(bf16)


def outer_kernel(scale, x_ref, z_ref, grad_ref, after, out_hbm, in_ref, made, sems):
    in_ref[...] = field_modes(scale, x_ref[0, 0], x_ref[0, 1], z_ref)
    del after
    lines, columns = made.shape[:2]
    across = 2
    size, unrolled = across * lines, 4
    groups = columns // across
    row = lax.broadcasted_iota(jnp.int32, (3 * size, LANES), 0) % size

    def copy(group):
        part = pl.ds(group * across, across)
        return pltpu.make_async_copy(made.at[:, part], out_hbm.at[:, part], sems.at[group])

    @pl.loop(0, groups // unrolled)
    def _(turn):
        for at in range(unrolled):
            group = turn * unrolled + at
            start = pl.multiple_of(group * size, size)
            in_high, in_low = split_twice(in_ref[pl.ds(start, size), :])
            high, low = split_twice(grad_ref[pl.ds(start, size), :])
            left = jnp.concatenate([in_high, in_low, in_high], 0)
            right = jnp.concatenate([high, high, low], 0)
            zero = jnp.zeros((), bf16)
            right = jnp.concatenate([jnp.where(row == mode, right, zero) for mode in range(size)], 1)
            every = lax.dot_general(
                left, right, (((0,), (0,)), ((), ())), preferred_element_type=f32
            )
            for mode in range(size):
                part = every[:, mode * LANES : (mode + 1) * LANES].astype(bf16)
                made[mode % lines, group * across + mode // lines] = part
            copy(group).start()

    @pl.loop(0, groups)
    def _(group):
        copy(group).wait()


def back_plane_kernel(s, scale, x_ref, first_ref, second_ref, sum_ref, out_ref):
    tiles = x_ref[...].astype(f32).reshape(s.gx, s.gy, 8, LANES)
    parts = jnp.concatenate(first_axis(tiles, first_ref, s.gx, s.gy), 1)
    rows, across = parts.shape
    wide = across // LANES
    turned = [parts]
    for turn in range(1, 4):
        moved = [
            pltpu.roll(parts[:, i * LANES : (i + 1) * LANES], turn * (LANES // 4), 1)
            for i in range(wide)
        ]
        turned.append(jnp.concatenate(moved, 1))
    high, low = split_twice(jnp.concatenate(turned, 0))
    table = second_ref[...]
    made = jnp.dot(
        jnp.concatenate([table, table], 1),
        jnp.concatenate([high, low], 0),
        preferred_element_type=f32,
    )
    group_of = lanes_of((rows, LANES)) // (LANES // 4)
    for part in range(wide):
        here = made[:, part * LANES : (part + 1) * LANES]
        value = here[:rows]
        for place in range(1, 4):
            value = jnp.where(group_of == place, here[place * rows : (place + 1) * rows], value)
        value = (value * scale).reshape(s.gy, 8, LANES)
        mine = slice(part * s.gy, (part + 1) * s.gy)
        out_ref[mine, :, :LANES] = value[:, :4].astype(bf16)
        out_ref[mine, :, LANES : 2 * LANES] = value[:, 4:].astype(bf16)
    sums = jnp.broadcast_to(sum_ref[...][None], (s.devices, 4, LANES))
    out_ref[:, :, 2 * LANES :] = sums.astype(bf16)


def close_kernel(scale, x_ref, z_ref, pre_ref, weight_ref, sum_ref, out_ref, skip_ref):
    pieces = quarters(x_ref[...].astype(f32)).astype(bf16)
    cells = jnp.dot(z_ref[...], pieces, preferred_element_type=f32)
    part = lax.dot_general(
        pre_ref[...], weight_ref[...], (((1,), (1,)), ((), ())), preferred_element_type=f32
    )
    out_ref[...] = (part + cells * scale).astype(bf16)
    skip_ref[...] = sum_ref[...].astype(f32)


def one_hot(rows, columns):
    return (np.asarray(rows)[:, None] == np.asarray(columns)[None, :]).astype(np.float32)


def twice(table):
    high = table.astype(np.float32).astype(bf16)
    low = (table - high.astype(np.float64)).astype(np.float32).astype(bf16)
    return np.concatenate([high, low], 1)


def make_tables(s):
    cas_x = plain_cas(s.x * s.gx, s.x * s.gx)
    cas_y = plain_cas(s.y * s.gy, s.y * s.gy)
    cas_z = plain_cas(s.z, s.z)
    norm = math.sqrt(s.x * s.gx * s.y * s.gy)
    t = {}
    t["first"] = twice(cas_x)
    t["back_first"] = twice(cas_x.T)
    count = s.gy * s.y // 2 * s.x
    py, yh, x = split_index(count, s.gy, s.y // 2, s.x)
    at = py * s.y + yh * 2
    same = one_hot(x, x)
    blocks = [cas_y[(at + b)[:, None], (at + y)[None, :]] * same for b, y in ((0, 0), (1, 1), (1, 0), (0, 1))]
    t["second"], factor = rounded_table(np.concatenate(blocks, 0))
    t["scale"] = factor / norm
    b, c, a = split_index(s.cells, s.y, s.z, s.x)
    bl, z, bh, al = split_index(s.cells, 2, s.z, s.y // 2, s.x)
    same = one_hot(a * s.y + b, al * s.y + bh * 2 + bl)
    t["z"] = same * cas_z[c[:, None], z[None, :]]
    t["z_scale"] = 1.0 / math.sqrt(s.z)
    py, x = split_index(s.gy * s.x, s.gy, s.x)
    same = one_hot(x, x)
    blocks = []
    for place in range(4):
        line = []
        for turn in range(4):
            at_y = py * s.y + place
            at_b = py * s.y + (place - turn) % 4
            line.append(cas_y[at_b[None, :], at_y[:, None]] * same)
        blocks.append(np.concatenate(line, 1))
    t["back_second"], factor = rounded_table(np.concatenate(blocks, 0))
    t["back_scale"] = factor / norm
    x, y, z = split_index(s.cells, s.x, s.y, s.z)
    yl, c, xl = split_index(s.cells, s.y, s.z, s.x)
    t["back_z"] = one_hot(x * s.y + y, xl * s.y + yl) * cas_z[c[None, :], z[:, None]]
    return {
        key: jnp.asarray(np.asarray(value, np.float32).astype(bf16))
        if isinstance(value, np.ndarray)
        else value
        for key, value in t.items()
    }


def call(kernel, out_shape, limit, flops, moved, **more):
    return pl.pallas_call(
        kernel,
        out_shape=out_shape,
        compiler_params=pltpu.CompilerParams(vmem_limit_bytes=limit * MIB),
        cost_estimate=pl.CostEstimate(flops=flops, bytes_accessed=moved, transcendentals=0),
        **more,
    )


def in_vmem(*shape, kind=bf16):
    return pltpu.VMEM(shape, kind)


def in_hbm(*shape, kind=bf16):
    return jax.ShapeDtypeStruct(shape, kind)


def exchange(pieces):
    return lax.all_to_all(pieces, ("gx", "gy"), 0, 0)


def on_device_whole_planes(s, inputs, preact, cotangent, spectral_w, skip_w):
    t = make_tables(s)
    cells, channels, devices = s.cells, s.channels, s.devices
    rows = cells // s.z // 2 * devices
    back_rows = devices * s.x
    flat = lambda array: array.reshape(cells, channels)
    vmem = pl.BlockSpec(memory_space=pltpu.VMEM)
    hbm = pl.BlockSpec(memory_space=pltpu.HBM)
    anywhere = pl.BlockSpec(memory_space=pl.ANY)
    field = pltpu.VMEM((cells, channels), bf16)
    pieces, grad_pre = call(
        functools.partial(open_kernel, s),
        (in_vmem(2, 2, cells // 2, LANES), in_vmem(cells, channels)),
        16,
        1 << 40,
        MIB,
        in_specs=[hbm] * 3,
        out_specs=(vmem, vmem),
        scratch_shapes=[field, field, field, pltpu.SemaphoreType.DMA((3,))],
    )(*(pltpu.with_memory_space_constraint(flat(a), pltpu.HBM) for a in (inputs, preact, cotangent)))
    columns = exchange(pieces.reshape(devices, -1, LANES))
    planes = call(
        functools.partial(plane_kernel, s, t["scale"]),
        in_vmem(rows, LANES),
        16,
        1 << 36,
        MIB,
        in_specs=[vmem] * 3,
        out_specs=vmem,
    )(columns.reshape(rows, LANES), t["first"], t["second"])
    owned = exchange(planes.reshape(devices, -1, LANES))
    owned = owned.reshape(2, 2, cells // 2, LANES)
    back, sums, grad_modes = call(
        functools.partial(modes_kernel, t["z_scale"]),
        (
            in_vmem(cells, channels),
            in_vmem(channels, channels),
            in_vmem(cells, channels, kind=f32),
        ),
        24,
        cells * channels * channels * 16,
        9 * MIB,
        in_specs=[vmem] * 5,
        out_specs=(vmem, vmem, vmem),
        scratch_shapes=[pltpu.VMEM((cells, channels), f32)],
    )(
        owned,
        t["z"],
        spectral_w.reshape(s.x, s.y * s.z, channels, channels),
        flat(inputs),
        grad_pre,
    )
    pieces = lambda rows, sums: jnp.concatenate(
        [rows[:, :4], rows[:, 4:], sums.reshape(devices, 4, channels)], 2
    )
    split = lambda got: (
        jnp.concatenate([got[:, :, :LANES], got[:, :, LANES : 2 * LANES]], 1).reshape(cells, LANES),
        got[:, :, 2 * LANES :],
    )
    back_columns, sums = split(exchange(pieces(back.reshape(devices, 8, LANES), sums)))
    skip_rows = jnp.sum(sums.astype(f32), 0) * (1.0 / math.sqrt(cells * devices))
    back_planes = call(
        functools.partial(back_plane_kernel, s, t["back_scale"]),
        in_hbm(devices, 4, 3 * LANES),
        16,
        back_rows * back_rows * LANES * 8,
        MIB,
        in_specs=[vmem] * 4,
        out_specs=vmem,
    )(back_columns, t["back_first"], t["back_second"], skip_rows)
    split_modes = (s.x, s.y * s.z, channels, channels)
    grad_spectral = call(
        functools.partial(outer_kernel, t["z_scale"]),
        in_hbm(*split_modes),
        24,
        cells * channels * channels * 2,
        9 * MIB,
        in_specs=[vmem] * 3 + [anywhere],
        out_specs=hbm,
        scratch_shapes=[
            pltpu.VMEM((cells, channels), f32),
            pltpu.VMEM(split_modes, bf16),
            pltpu.SemaphoreType.DMA((s.y * s.z // 2,)),
        ],
    )(owned, t["z"], grad_modes, back_planes)
    spectral, sums = split(exchange(back_planes))
    grad_inputs, grad_skip = call(
        functools.partial(close_kernel, t["z_scale"]),
        (in_hbm(cells, channels), in_hbm(channels, channels, kind=f32)),
        16,
        cells * cells * LANES * 4,
        MIB,
        in_specs=[vmem] * 5,
        out_specs=(vmem, vmem),
    )(spectral, t["back_z"], grad_pre, skip_w, sums.reshape(channels, channels))
    return (
        grad_inputs.reshape(inputs.shape),
        grad_spectral.reshape(spectral_w.shape),
        grad_skip,
    )


def on_device(inputs, preact, cotangent, spectral_w, skip_w):
    sizes = Sizes(inputs, spectral_w, lax.axis_size("gx"), lax.axis_size("gy"))
    if sizes.fits(inputs, spectral_w):
        return on_device_whole_planes(sizes, inputs, preact, cotangent, spectral_w, skip_w)
    return on_device_any(inputs, preact, cotangent, spectral_w, skip_w)


def on_device_any(inputs, preact, cotangent, spectral_w, skip_w):
    cells_x, cells_y, cells_z, channels = inputs.shape
    length_x = cells_x * lax.axis_size("gx")
    length_y = cells_y * lax.axis_size("gy")
    local_modes_x, local_modes_y, modes_z = (
        spectral_w.shape[0],
        spectral_w.shape[1],
        spectral_w.shape[2],
    )
    modes_x = local_modes_x * lax.axis_size("gx")
    modes_y = local_modes_y * lax.axis_size("gy")
    table_z = cas_table(modes_z, cells_z, 0, cells_z)
    table_x = cas_table(modes_x, length_x, lax.axis_index("gx") * cells_x, cells_x)
    table_y = cas_table(modes_y, length_y, lax.axis_index("gy") * cells_y, cells_y)
    preact_wide = preact.astype(jnp.float32)
    gelu_slope = 0.5 * (
        1.0 + lax.erf(preact_wide * (1.0 / math.sqrt(2.0)))
    ) + preact_wide * jnp.exp(-0.5 * preact_wide * preact_wide) * (1.0 / math.sqrt(2.0 * math.pi))
    grad_pre = (cotangent.astype(jnp.float32) * gelu_slope).astype(jnp.bfloat16)
    fields = jnp.stack([inputs, grad_pre]).astype(jnp.float32)
    z_modes = jnp.einsum("ck,fijkh->fijch", table_z, fields, precision=highest)
    table_rows = table_y
    part_y = lax.psum_scatter(
        jnp.einsum("bj,fijch->bfich", table_rows, z_modes, precision=highest),
        "gy",
        scatter_dimension=0,
        tiled=True,
    )
    table_rows = table_x
    owned_modes = lax.psum_scatter(
        jnp.einsum("ai,bfich->abfch", table_rows, part_y, precision=highest),
        "gx",
        scatter_dimension=0,
        tiled=True,
    )
    input_modes = owned_modes[:, :, 0]
    grad_modes = owned_modes[:, :, 1]
    grad_spectral = jnp.einsum(
        "abcp,abcq->abcpq", input_modes, grad_modes, precision=highest
    ).astype(jnp.bfloat16)
    back_modes = jnp.einsum(
        "abcq,abcpq->abcp", grad_modes, spectral_w.astype(jnp.float32), precision=highest
    ).astype(jnp.bfloat16)
    table_rows = table_x
    over_first = jnp.einsum(
        "ai,abch->ibch",
        table_rows,
        lax.all_gather(back_modes, "gx", axis=0, tiled=True).astype(jnp.float32),
        precision=highest,
    )
    table_rows = table_y
    cell_modes = jnp.einsum(
        "bj,ibch->ijch",
        table_rows,
        lax.all_gather(over_first, "gy", axis=1, tiled=True),
        precision=highest,
    )
    spectral_cells = jnp.einsum("ck,ijch->ijkh", table_z, cell_modes, precision=highest)
    flat_grad = grad_pre.reshape(-1, channels)
    skip_part = lax.dot_general(
        flat_grad, skip_w, (((1,), (1,)), ((), ())), preferred_element_type=jnp.float32
    )
    grad_inputs = (skip_part.reshape(cells_x, cells_y, cells_z, channels) + spectral_cells).astype(
        jnp.bfloat16
    )
    local_sum = lax.dot_general(
        inputs.reshape(-1, channels),
        flat_grad,
        (((0,), (0,)), ((), ())),
        preferred_element_type=jnp.float32,
    )
    grad_skip = lax.psum(local_sum, ("gx", "gy")) / math.sqrt(length_x * length_y * cells_z)
    return (grad_inputs, grad_spectral, grad_skip)


def solution(mesh):
    in_specs = (
        P("gx", "gy", None, None),
        P("gx", "gy", None, None),
        P("gx", "gy", None, None),
        P("gx", "gy", None, None, None),
        P(),
    )
    out_specs = (P("gx", "gy", None, None), P("gx", "gy", None, None, None), P())
    return jax.shard_map(
        on_device, mesh=mesh, in_specs=in_specs, out_specs=out_specs, check_vma=False
    )
```

```python
import functools
import math

import jax
import jax.numpy as jnp
import numpy as np
from jax import lax
from jax.experimental import pallas as pl
from jax.experimental.pallas import tpu as pltpu
from jax.sharding import PartitionSpec as P

highest = lax.Precision.HIGHEST
f32 = jnp.float32
bf16 = jnp.bfloat16
LANES = 128
MIB = 1 << 20


def cas_table(modes, length, offset, cells):
    index = jnp.arange(modes, dtype=jnp.int32)
    freq = jnp.where(index < modes // 2, index, length - modes + index)
    where_cells = offset + jnp.arange(cells, dtype=jnp.int32)
    phase = freq[:, None] * where_cells[None, :] % length
    angle = phase.astype(jnp.float32) * (2.0 * math.pi / length)
    return (jnp.cos(angle) + jnp.sin(angle)) / math.sqrt(length)


def gelu_slope_of(preact_wide):
    return 0.5 * (
        1.0 + lax.erf(preact_wide * (1.0 / math.sqrt(2.0)))
    ) + preact_wide * jnp.exp(-0.5 * preact_wide * preact_wide) * (1.0 / math.sqrt(2.0 * math.pi))


def plain_cas(modes, length):
    index = np.arange(modes)
    freq = np.where(index < modes // 2, index, length - modes + index)
    angle = 2.0 * np.pi * ((freq[:, None] * np.arange(length)[None, :]) % length) / length
    return np.cos(angle) + np.sin(angle)


def rounded_table(table):
    values, counts = np.unique(np.round(np.abs(table), 12), return_counts=True)
    best = None
    for scale in np.linspace(1.0, 2.0, 512, endpoint=False):
        kept = (values * scale).astype(np.float32).astype(bf16).astype(np.float64) / scale
        error = np.sum(counts * (kept - values) ** 2)
        if best is None or error < best[0]:
            best = (error, scale)
    return (table * best[1]).astype(np.float32).astype(bf16), 1.0 / best[1]


def split_index(size, *parts):
    return np.unravel_index(np.arange(size), parts)


class Sizes:
    def __init__(self, inputs, spectral_w, gx, gy):
        self.gx, self.gy = gx, gy
        self.devices = gx * gy
        self.x, self.y, self.z, self.channels = inputs.shape
        self.cells = self.x * self.y * self.z
        self.width = 2 * self.z * self.channels // self.devices
        self.back_width = self.z * self.channels // self.devices

    def fits(self, inputs, spectral_w):
        if inputs.shape[:3] != spectral_w.shape[:3] or self.channels != LANES:
            return False
        if self.back_width * 4 != LANES or self.y % 4:
            return False
        rows = self.x * self.y // 2
        return rows == 16 and self.devices * 4 == LANES and self.x * self.y // 4 == 8 and self.z == 8


def lanes_of(shape):
    return lax.broadcasted_iota(jnp.int32, shape, len(shape) - 1)


def load(*pairs):
    copies = [pltpu.make_async_copy(source, target, sem) for source, target, sem in pairs]
    for copy in copies:
        copy.start()
    return copies


def open_kernel(s, in_hbm, pre_hbm, cot_hbm, pack_ref, grad_ref, in_ref, pre_ref, cot_ref, sems):
    copies = load(
        (in_hbm, in_ref, sems.at[0]),
        (pre_hbm, pre_ref, sems.at[1]),
        (cot_hbm, cot_ref, sems.at[2]),
    )
    cells = s.cells
    place = lax.broadcasted_iota(jnp.int32, (cells, 1), 0)
    half_y, half = s.y // 2, cells // 2
    yl, rest = place // half, place % half
    mode, rest = rest // (s.x * half_y), rest % (s.x * half_y)
    yh, x = rest // s.x, rest % s.x
    source = lax.broadcasted_iota(jnp.int32, (1, cells), 1)
    phase = mode * (source % s.z) % s.z
    table = jnp.zeros((cells, cells), f32)
    for value in range(s.z):
        angle = 2.0 * math.pi * value / s.z
        table = jnp.where(phase == value, math.cos(angle) + math.sin(angle), table)
    table = jnp.where(x * s.y + yh * 2 + yl == source // s.z, table, 0.0).astype(bf16)
    for copy in copies:
        copy.wait()
    grad = (cot_ref[...].astype(f32) * gelu_slope_of(pre_ref[...].astype(f32))).astype(bf16)
    grad_ref[...] = grad
    rows = jnp.dot(
        table, jnp.concatenate([in_ref[...], grad], 1), preferred_element_type=f32
    )
    width = LANES // 2
    half = rows.shape[0] // 2
    low = lanes_of((half, LANES)) < width
    for field in range(2):
        even = rows[:half, field * LANES : (field + 1) * LANES]
        odd = rows[half:, field * LANES : (field + 1) * LANES]
        pack_ref[field, 0] = jnp.where(low, even, pltpu.roll(odd, width, 1)).astype(bf16)
        pack_ref[field, 1] = jnp.where(low, pltpu.roll(even, width, 1), odd).astype(bf16)


def first_axis(tiles, table_ref, along, across):
    lines = [tiles[:, j].reshape(along * 8, LANES) for j in range(across)]
    lines = jnp.concatenate(lines, 1).astype(bf16)
    made = jnp.dot(
        table_ref[...], jnp.concatenate([lines, lines], 0), preferred_element_type=f32
    )
    return [
        jnp.concatenate(
            [made[i * 8 : i * 8 + 8, j * LANES : (j + 1) * LANES] for j in range(across)], 0
        )
        for i in range(along)
    ]


def plane_kernel(s, scale, x_ref, first_ref, second_ref, out_ref):
    width = LANES // 2
    across = s.gy * s.y // 2
    tiles = x_ref[...].astype(f32).reshape(s.gx, across, 8, LANES)
    parts = jnp.concatenate(first_axis(tiles, first_ref, s.gx, across), 1)
    rows = across * 8
    table = second_ref[...]
    made = jnp.dot(
        jnp.concatenate([table, table], 1),
        jnp.concatenate(split_twice(parts), 0),
        preferred_element_type=f32,
    )
    low = lanes_of((rows, LANES)) < width
    for part in range(s.gx):
        here = made[:, part * LANES : (part + 1) * LANES]
        straight = jnp.where(low, here[:rows], here[rows : 2 * rows])
        crossed = jnp.where(low, here[2 * rows : 3 * rows], here[3 * rows :])
        value = (straight + pltpu.roll(crossed, width, 1)) * scale
        out_ref[part * rows : (part + 1) * rows, :] = value.astype(bf16)


def field_modes(s, first, second):
    width = LANES // 2
    first, second = first.astype(f32), second.astype(f32)
    low = lanes_of(first.shape) < width
    even = jnp.where(low, first, pltpu.roll(second, width, 1))
    odd = jnp.where(low, pltpu.roll(first, width, 1), second)
    even, odd = (value.reshape(s.z, s.y // 2, s.x, LANES) for value in (even, odd))
    lines = [value[:, half].reshape(s.z * s.x, LANES) for half in range(s.y // 2) for value in (even, odd)]
    return jnp.concatenate(lines, 0)


def split_twice(value):
    high = value.astype(bf16)
    return high, (value - high.astype(f32)).astype(bf16)


def quarters(rows):
    quarter = rows.shape[0] // 4
    group_of = lanes_of((quarter, LANES)) // (LANES // 4)
    pieces = []
    for part in range(4):
        piece = rows[:quarter]
        for place in range(4):
            source = rows[place * quarter : (place + 1) * quarter]
            turn = (place - part) % 4
            moved = source if turn == 0 else pltpu.roll(source, turn * (LANES // 4), 1)
            piece = jnp.where(group_of == place, moved, piece)
        pieces.append(piece)
    return jnp.concatenate(pieces, 0)


def modes_kernel(s, x_ref, w_ref, field_ref, pre_ref, pack_ref, modes_ref, back):
    sums = lax.dot_general(
        field_ref[...], pre_ref[...], (((0,), (0,)), ((), ())), preferred_element_type=f32
    )
    pack_ref[:, :, 2 * LANES :] = sums.reshape(s.devices, 4, LANES).astype(bf16)
    modes_ref[...] = field_modes(s, x_ref[1, 0], x_ref[1, 1])
    groups = modes_ref.shape[0] // 8
    row = lax.broadcasted_iota(jnp.int32, (8, LANES), 0)
    lane = lanes_of((LANES, LANES))
    on_vector = [group for group in range(groups) if group * 10 // groups != (group + 1) * 10 // groups]
    kept = jnp.zeros((LANES, LANES), f32)
    for group in range(groups):
        start = group * 8
        if group in on_vector:
            for mode in range(8):
                weights = w_ref[mode, group].astype(f32)
                total = jnp.sum(weights * modes_ref[start + mode : start + mode + 1, :], 1, keepdims=True)
                kept = jnp.where(lane == on_vector.index(group) * 8 + mode, total, kept)
            continue
        every = lax.dot_general(
            modes_ref[start : start + 8, :].astype(bf16),
            w_ref[:, group].reshape(8 * LANES, LANES),
            (((1,), (1,)), ((), ())),
            preferred_element_type=f32,
        )
        total = jnp.zeros((8, LANES), f32)
        for mode in range(8):
            total = jnp.where(row == mode, every[:, mode * LANES : (mode + 1) * LANES], total)
        back[start : start + 8, :] = total
    kept = kept.T
    for at, group in enumerate(on_vector):
        back[group * 8 : group * 8 + 8, :] = kept[at * 8 : at * 8 + 8]

    rows = back[...].astype(bf16).astype(f32)
    rows = quarters(rows).reshape(s.devices, 8, LANES)
    pack_ref[:, :, :LANES] = rows[:, :4].astype(bf16)
    pack_ref[:, :, LANES : 2 * LANES] = rows[:, 4:].astype(bf16)


def outer_kernel(s, x_ref, grad_ref, pre_ref, weight_ref, after, out_hbm, part_ref, in_ref, made, sems):
    del after
    in_ref[...] = field_modes(s, x_ref[0, 0], x_ref[0, 1])
    lines, columns = made.shape[:2]
    across = 2
    size, unrolled = across * lines, 4
    groups = columns // across
    row = lax.broadcasted_iota(jnp.int32, (size, LANES), 0)

    def copy(group):
        part = pl.ds(group * across, across)
        return pltpu.make_async_copy(made.at[:, part], out_hbm.at[:, part], sems.at[group])

    @pl.loop(0, groups // unrolled)
    def _(turn):
        for at in range(unrolled):
            group = turn * unrolled + at
            start = pl.multiple_of(group * size, size)
            left = in_ref[pl.ds(start, size), :].astype(bf16)
            right = grad_ref[pl.ds(start, size), :].astype(bf16)
            zero = jnp.zeros((), bf16)
            right = jnp.concatenate([jnp.where(row == mode, right, zero) for mode in range(size)], 1)
            every = lax.dot_general(
                left, right, (((0,), (0,)), ((), ())), preferred_element_type=f32
            )
            for mode in range(size):
                part = every[:, mode * LANES : (mode + 1) * LANES].astype(bf16)
                made[mode % lines, group * across + mode // lines] = part
            copy(group).start()

    part_ref[...] = lax.dot_general(
        pre_ref[...], weight_ref[...], (((1,), (1,)), ((), ())), preferred_element_type=f32
    )

    @pl.loop(0, groups)
    def _(group):
        copy(group).wait()


def opened(got_ref):
    got = [got_ref[:, :, i * LANES : (i + 1) * LANES].astype(f32) for i in range(3)]
    return jnp.concatenate(got[:2], 1), got[2]


def back_plane_kernel(s, scale, skip_scale, got_ref, first_ref, second_ref, out_ref):
    tiles, sums = opened(got_ref)
    tiles = tiles.reshape(s.gx, s.gy, 8, LANES)
    parts = jnp.concatenate(first_axis(tiles, first_ref, s.gx, s.gy), 1)
    rows, across = parts.shape
    wide = across // LANES
    turned = [parts]
    for turn in range(1, 4):
        moved = [
            pltpu.roll(parts[:, i * LANES : (i + 1) * LANES], turn * (LANES // 4), 1)
            for i in range(wide)
        ]
        turned.append(jnp.concatenate(moved, 1))
    high, low = split_twice(jnp.concatenate(turned, 0))
    table = second_ref[...]
    made = jnp.dot(
        jnp.concatenate([table, table], 1),
        jnp.concatenate([high, low], 0),
        preferred_element_type=f32,
    )
    group_of = lanes_of((rows, LANES)) // (LANES // 4)
    for part in range(wide):
        here = made[:, part * LANES : (part + 1) * LANES]
        value = here[:rows]
        for place in range(1, 4):
            value = jnp.where(group_of == place, here[place * rows : (place + 1) * rows], value)
        value = (value * scale).reshape(s.gy, 8, LANES)
        mine = slice(part * s.gy, (part + 1) * s.gy)
        out_ref[mine, :, :LANES] = value[:, :4].astype(bf16)
        out_ref[mine, :, LANES : 2 * LANES] = value[:, 4:].astype(bf16)
    sums = jnp.sum(sums, 0, keepdims=True) * skip_scale
    out_ref[:, :, 2 * LANES :] = jnp.broadcast_to(sums, (s.devices, 4, LANES)).astype(bf16)


def close_kernel(scale, got_ref, z_ref, part_ref, out_ref, skip_ref):
    rows, sums = opened(got_ref)
    skip_ref[...] = sums
    pieces = quarters(rows.reshape(-1, LANES)).astype(bf16)
    cells = jnp.dot(z_ref[...], pieces, preferred_element_type=f32)
    out_ref[...] = (part_ref[...] + cells * scale).astype(bf16)


def one_hot(rows, columns):
    return (np.asarray(rows)[:, None] == np.asarray(columns)[None, :]).astype(np.float32)


def twice(table):
    high = table.astype(np.float32).astype(bf16)
    low = (table - high.astype(np.float64)).astype(np.float32).astype(bf16)
    return np.concatenate([high, low], 1)


def make_tables(s):
    cas_x = plain_cas(s.x * s.gx, s.x * s.gx)
    cas_y = plain_cas(s.y * s.gy, s.y * s.gy)
    cas_z = plain_cas(s.z, s.z)
    norm = math.sqrt(s.x * s.gx * s.y * s.gy)
    t = {}
    t["first"] = twice(cas_x)
    t["back_first"] = twice(cas_x.T)
    count = s.gy * s.y // 2 * s.x
    py, yh, x = split_index(count, s.gy, s.y // 2, s.x)
    at = py * s.y + yh * 2
    same = one_hot(x, x)
    blocks = [cas_y[(at + b)[:, None], (at + y)[None, :]] * same for b, y in ((0, 0), (1, 1), (1, 0), (0, 1))]
    t["second"], factor = rounded_table(np.concatenate(blocks, 0))
    t["scale"] = factor / norm
    t["z_scale"] = 1.0 / math.sqrt(s.z)
    py, x = split_index(s.gy * s.x, s.gy, s.x)
    same = one_hot(x, x)
    blocks = []
    for place in range(4):
        line = []
        for turn in range(4):
            at_y = py * s.y + place
            at_b = py * s.y + (place - turn) % 4
            line.append(cas_y[at_b[None, :], at_y[:, None]] * same)
        blocks.append(np.concatenate(line, 1))
    t["back_second"], factor = rounded_table(np.concatenate(blocks, 0))
    t["back_scale"] = factor / norm
    x, y, z = split_index(s.cells, s.x, s.y, s.z)
    yl, c, xl = split_index(s.cells, s.y, s.z, s.x)
    t["back_z"] = one_hot(x * s.y + y, xl * s.y + yl) * cas_z[c[None, :], z[:, None]]
    return {
        key: jnp.asarray(np.asarray(value, np.float32).astype(bf16))
        if isinstance(value, np.ndarray)
        else value
        for key, value in t.items()
    }


def call(kernel, out_shape, limit, flops, moved, **more):
    return pl.pallas_call(
        kernel,
        out_shape=out_shape,
        compiler_params=pltpu.CompilerParams(vmem_limit_bytes=limit * MIB),
        cost_estimate=pl.CostEstimate(flops=flops, bytes_accessed=moved, transcendentals=0),
        **more,
    )


def in_vmem(*shape, kind=bf16):
    return pltpu.VMEM(shape, kind)


def in_hbm(*shape, kind=bf16):
    return jax.ShapeDtypeStruct(shape, kind)


def exchange(pieces):
    return lax.all_to_all(pieces, ("gx", "gy"), 0, 0)


def on_device_whole_planes(s, inputs, preact, cotangent, spectral_w, skip_w):
    t = make_tables(s)
    cells, channels, devices = s.cells, s.channels, s.devices
    rows = cells // s.z // 2 * devices
    back_rows = devices * s.x
    flat = lambda array: array.reshape(cells, channels)
    vmem = pl.BlockSpec(memory_space=pltpu.VMEM)
    hbm = pl.BlockSpec(memory_space=pltpu.HBM)
    anywhere = pl.BlockSpec(memory_space=pl.ANY)
    field = pltpu.VMEM((cells, channels), bf16)
    given = (flat(inputs), flat(preact), flat(cotangent))
    pieces, grad_pre = call(
        functools.partial(open_kernel, s),
        (in_vmem(2, 2, cells // 2, LANES), in_vmem(cells, channels)),
        16,
        1 << 40,
        MIB,
        in_specs=[hbm] * 3,
        out_specs=(vmem, vmem),
        scratch_shapes=[field, field, field, pltpu.SemaphoreType.DMA((3,))],
    )(*(pltpu.with_memory_space_constraint(a, pltpu.HBM) for a in given))
    columns = exchange(pieces.reshape(devices, -1, LANES))
    planes = call(
        functools.partial(plane_kernel, s, t["scale"] * t["z_scale"]),
        in_vmem(rows, LANES),
        16,
        1 << 36,
        MIB,
        in_specs=[vmem] * 3,
        out_specs=vmem,
    )(columns.reshape(rows, LANES), t["first"], t["second"])
    owned = exchange(planes.reshape(devices, -1, LANES))
    owned = owned.reshape(2, 2, cells // 2, LANES)
    back, grad_modes = call(
        functools.partial(modes_kernel, s),
        (
            in_vmem(devices, 4, 3 * LANES),
            in_vmem(cells, channels, kind=f32),
        ),
        24,
        cells * channels * channels * 16,
        9 * MIB,
        in_specs=[vmem] * 4,
        out_specs=(vmem, vmem),
        scratch_shapes=[pltpu.VMEM((cells, channels), f32)],
    )(
        owned,
        spectral_w.reshape(s.x, s.y * s.z, channels, channels),
        flat(inputs),
        grad_pre,
    )
    got = exchange(back)
    back_planes = call(
        functools.partial(
            back_plane_kernel, s, t["back_scale"], 1.0 / math.sqrt(cells * devices)
        ),
        in_hbm(devices, 4, 3 * LANES),
        16,
        back_rows * back_rows * LANES * 8,
        MIB,
        in_specs=[vmem] * 3,
        out_specs=vmem,
    )(got, t["back_first"], t["back_second"])
    split_modes = (s.x, s.y * s.z, channels, channels)
    split_modes = (s.x, s.y * s.z, channels, channels)
    grad_spectral, skip_part = call(
        functools.partial(outer_kernel, s),
        (in_hbm(*split_modes), in_vmem(cells, channels, kind=f32)),
        24,
        cells * channels * channels * 2,
        9 * MIB,
        in_specs=[vmem] * 4 + [anywhere],
        out_specs=(hbm, vmem),
        scratch_shapes=[
            pltpu.VMEM((cells, channels), f32),
            pltpu.VMEM(split_modes, bf16),
            pltpu.SemaphoreType.DMA((s.y * s.z // 2,)),
        ],
    )(owned, grad_modes, grad_pre, skip_w, back_planes)
    got = exchange(back_planes)
    grad_inputs, grad_skip = call(
        functools.partial(close_kernel, t["z_scale"]),
        (in_hbm(cells, channels), in_hbm(devices, 4, channels, kind=f32)),
        16,
        cells * cells * LANES * 4,
        MIB,
        in_specs=[vmem] * 3,
        out_specs=(vmem, vmem),
    )(got, t["back_z"], skip_part)
    return (
        grad_inputs.reshape(inputs.shape),
        grad_spectral.reshape(spectral_w.shape),
        grad_skip.reshape(channels, channels),
    )


def on_device(inputs, preact, cotangent, spectral_w, skip_w):
    sizes = Sizes(inputs, spectral_w, lax.axis_size("gx"), lax.axis_size("gy"))
    if sizes.fits(inputs, spectral_w):
        return on_device_whole_planes(sizes, inputs, preact, cotangent, spectral_w, skip_w)
    return on_device_any(inputs, preact, cotangent, spectral_w, skip_w)


def on_device_any(inputs, preact, cotangent, spectral_w, skip_w):
    cells_x, cells_y, cells_z, channels = inputs.shape
    length_x = cells_x * lax.axis_size("gx")
    length_y = cells_y * lax.axis_size("gy")
    local_modes_x, local_modes_y, modes_z = (
        spectral_w.shape[0],
        spectral_w.shape[1],
        spectral_w.shape[2],
    )
    modes_x = local_modes_x * lax.axis_size("gx")
    modes_y = local_modes_y * lax.axis_size("gy")
    table_z = cas_table(modes_z, cells_z, 0, cells_z)
    table_x = cas_table(modes_x, length_x, lax.axis_index("gx") * cells_x, cells_x)
    table_y = cas_table(modes_y, length_y, lax.axis_index("gy") * cells_y, cells_y)
    preact_wide = preact.astype(jnp.float32)
    gelu_slope = 0.5 * (
        1.0 + lax.erf(preact_wide * (1.0 / math.sqrt(2.0)))
    ) + preact_wide * jnp.exp(-0.5 * preact_wide * preact_wide) * (1.0 / math.sqrt(2.0 * math.pi))
    grad_pre = (cotangent.astype(jnp.float32) * gelu_slope).astype(jnp.bfloat16)
    fields = jnp.stack([inputs, grad_pre]).astype(jnp.float32)
    z_modes = jnp.einsum("ck,fijkh->fijch", table_z, fields, precision=highest)
    table_rows = table_y
    part_y = lax.psum_scatter(
        jnp.einsum("bj,fijch->bfich", table_rows, z_modes, precision=highest),
        "gy",
        scatter_dimension=0,
        tiled=True,
    )
    table_rows = table_x
    owned_modes = lax.psum_scatter(
        jnp.einsum("ai,bfich->abfch", table_rows, part_y, precision=highest),
        "gx",
        scatter_dimension=0,
        tiled=True,
    )
    input_modes = owned_modes[:, :, 0]
    grad_modes = owned_modes[:, :, 1]
    grad_spectral = jnp.einsum(
        "abcp,abcq->abcpq", input_modes, grad_modes, precision=highest
    ).astype(jnp.bfloat16)
    back_modes = jnp.einsum(
        "abcq,abcpq->abcp", grad_modes, spectral_w.astype(jnp.float32), precision=highest
    ).astype(jnp.bfloat16)
    table_rows = table_x
    over_first = jnp.einsum(
        "ai,abch->ibch",
        table_rows,
        lax.all_gather(back_modes, "gx", axis=0, tiled=True).astype(jnp.float32),
        precision=highest,
    )
    table_rows = table_y
    cell_modes = jnp.einsum(
        "bj,ibch->ijch",
        table_rows,
        lax.all_gather(over_first, "gy", axis=1, tiled=True),
        precision=highest,
    )
    spectral_cells = jnp.einsum("ck,ijch->ijkh", table_z, cell_modes, precision=highest)
    flat_grad = grad_pre.reshape(-1, channels)
    skip_part = lax.dot_general(
        flat_grad, skip_w, (((1,), (1,)), ((), ())), preferred_element_type=jnp.float32
    )
    grad_inputs = (skip_part.reshape(cells_x, cells_y, cells_z, channels) + spectral_cells).astype(
        jnp.bfloat16
    )
    local_sum = lax.dot_general(
        inputs.reshape(-1, channels),
        flat_grad,
        (((0,), (0,)), ((), ())),
        preferred_element_type=jnp.float32,
    )
    grad_skip = lax.psum(local_sum, ("gx", "gy")) / math.sqrt(length_x * length_y * cells_z)
    return (grad_inputs, grad_spectral, grad_skip)


def solution(mesh):
    in_specs = (
        P("gx", "gy", None, None),
        P("gx", "gy", None, None),
        P("gx", "gy", None, None),
        P("gx", "gy", None, None, None),
        P(),
    )
    out_specs = (P("gx", "gy", None, None), P("gx", "gy", None, None, None), P())
    return jax.shard_map(
        on_device, mesh=mesh, in_specs=in_specs, out_specs=out_specs, check_vma=False
    )
```

```python
import functools
import math

import jax
import jax.numpy as jnp
import numpy as np
from jax import lax
from jax.experimental import pallas as pl
from jax.experimental.pallas import tpu as pltpu
from jax.sharding import PartitionSpec as P

highest = lax.Precision.HIGHEST
f32 = jnp.float32
bf16 = jnp.bfloat16
LANES = 128
MIB = 1 << 20


def cas_table(modes, length, offset, cells):
    index = jnp.arange(modes, dtype=jnp.int32)
    freq = jnp.where(index < modes // 2, index, length - modes + index)
    where_cells = offset + jnp.arange(cells, dtype=jnp.int32)
    phase = freq[:, None] * where_cells[None, :] % length
    angle = phase.astype(jnp.float32) * (2.0 * math.pi / length)
    return (jnp.cos(angle) + jnp.sin(angle)) / math.sqrt(length)


def gelu_slope_of(preact_wide):
    return 0.5 * (
        1.0 + lax.erf(preact_wide * (1.0 / math.sqrt(2.0)))
    ) + preact_wide * jnp.exp(-0.5 * preact_wide * preact_wide) * (1.0 / math.sqrt(2.0 * math.pi))


def plain_cas(modes, length):
    index = np.arange(modes)
    freq = np.where(index < modes // 2, index, length - modes + index)
    angle = 2.0 * np.pi * ((freq[:, None] * np.arange(length)[None, :]) % length) / length
    return np.cos(angle) + np.sin(angle)


def rounded_table(table):
    values, counts = np.unique(np.round(np.abs(table), 12), return_counts=True)
    best = None
    for scale in np.linspace(1.0, 2.0, 512, endpoint=False):
        kept = (values * scale).astype(np.float32).astype(bf16).astype(np.float64) / scale
        error = np.sum(counts * (kept - values) ** 2)
        if best is None or error < best[0]:
            best = (error, scale)
    return (table * best[1]).astype(np.float32).astype(bf16), 1.0 / best[1]


def split_index(size, *parts):
    return np.unravel_index(np.arange(size), parts)


class Sizes:
    def __init__(self, inputs, spectral_w, gx, gy):
        self.gx, self.gy = gx, gy
        self.devices = gx * gy
        self.x, self.y, self.z, self.channels = inputs.shape
        self.cells = self.x * self.y * self.z
        self.width = 2 * self.z * self.channels // self.devices
        self.back_width = self.z * self.channels // self.devices

    def fits(self, inputs, spectral_w):
        if inputs.shape[:3] != spectral_w.shape[:3] or self.channels != LANES:
            return False
        if self.back_width * 4 != LANES or self.y % 4:
            return False
        rows = self.x * self.y // 2
        return rows == 16 and self.devices * 4 == LANES and self.x * self.y // 4 == 8 and self.z == 8


def lanes_of(shape):
    return lax.broadcasted_iota(jnp.int32, shape, len(shape) - 1)


def load(*pairs):
    copies = [pltpu.make_async_copy(source, target, sem) for source, target, sem in pairs]
    for copy in copies:
        copy.start()
    return copies


def open_kernel(s, in_hbm, pre_hbm, cot_hbm, pack_ref, grad_ref, in_ref, pre_ref, cot_ref, sems):
    copies = load(
        (in_hbm, in_ref, sems.at[0]),
        (pre_hbm, pre_ref, sems.at[1]),
        (cot_hbm, cot_ref, sems.at[2]),
    )
    cells = s.cells
    place = lax.broadcasted_iota(jnp.int32, (cells, 1), 0)
    half_y, half = s.y // 2, cells // 2
    yl, rest = place // half, place % half
    mode, rest = rest // (s.x * half_y), rest % (s.x * half_y)
    yh, x = rest // s.x, rest % s.x
    source = lax.broadcasted_iota(jnp.int32, (1, cells), 1)
    phase = mode * (source % s.z) % s.z
    table = jnp.zeros((cells, cells), f32)
    for value in range(s.z):
        angle = 2.0 * math.pi * value / s.z
        table = jnp.where(phase == value, math.cos(angle) + math.sin(angle), table)
    table = jnp.where(x * s.y + yh * 2 + yl == source // s.z, table, 0.0).astype(bf16)
    for copy in copies:
        copy.wait()
    grad = (cot_ref[...].astype(f32) * gelu_slope_of(pre_ref[...].astype(f32))).astype(bf16)
    grad_ref[...] = grad
    rows = jnp.dot(
        table, jnp.concatenate([in_ref[...], grad], 1), preferred_element_type=f32
    )
    width = LANES // 2
    half = rows.shape[0] // 2
    low = lanes_of((half, LANES)) < width
    for field in range(2):
        even = rows[:half, field * LANES : (field + 1) * LANES]
        odd = rows[half:, field * LANES : (field + 1) * LANES]
        pack_ref[field, 0] = jnp.where(low, even, pltpu.roll(odd, width, 1)).astype(bf16)
        pack_ref[field, 1] = jnp.where(low, pltpu.roll(even, width, 1), odd).astype(bf16)


def first_axis(tiles, table_ref, along, across):
    lines = [tiles[:, j].reshape(along * 8, LANES) for j in range(across)]
    lines = jnp.concatenate(lines, 1).astype(bf16)
    made = jnp.dot(
        table_ref[...], jnp.concatenate([lines, lines], 0), preferred_element_type=f32
    )
    return [
        jnp.concatenate(
            [made[i * 8 : i * 8 + 8, j * LANES : (j + 1) * LANES] for j in range(across)], 0
        )
        for i in range(along)
    ]


def halves(first, second):
    width = LANES // 2
    low = lanes_of(first.shape) < width
    return (
        jnp.where(low, first, pltpu.roll(second, width, 1)),
        jnp.where(low, pltpu.roll(first, width, 1), second),
    )


def second_axis(table_ref, value):
    table = table_ref[...]
    return jnp.dot(
        jnp.concatenate([table, table], 1),
        jnp.concatenate(split_twice(value), 0),
        preferred_element_type=f32,
    )


def plane_kernel(s, scale, x_ref, first_ref, second_ref, out_ref):
    across = s.gy * s.y // 2
    tiles = x_ref[...].astype(f32).reshape(s.gx, across, 8, LANES)
    parts = first_axis(tiles, first_ref, s.gx, across)
    pairs = [jnp.concatenate(halves(*parts[i : i + 2]), 0) for i in range(0, s.gx, 2)]
    made = second_axis(second_ref, jnp.concatenate(pairs, 1)) * scale
    rows = across * 8
    for pair in range(s.gx // 2):
        here = made[:, pair * LANES : (pair + 1) * LANES]
        for i, value in enumerate(halves(here[:rows], here[rows:])):
            start = (pair * 2 + i) * rows
            out_ref[start : start + rows, :] = value.astype(bf16)


def field_modes(s, first, second):
    width = LANES // 2
    first, second = first.astype(f32), second.astype(f32)
    low = lanes_of(first.shape) < width
    even = jnp.where(low, first, pltpu.roll(second, width, 1))
    odd = jnp.where(low, pltpu.roll(first, width, 1), second)
    even, odd = (value.reshape(s.z, s.y // 2, s.x, LANES) for value in (even, odd))
    lines = [value[:, half].reshape(s.z * s.x, LANES) for half in range(s.y // 2) for value in (even, odd)]
    return jnp.concatenate(lines, 0)


def split_twice(value):
    high = value.astype(bf16)
    return high, (value - high.astype(f32)).astype(bf16)


def quarters(rows):
    quarter = rows.shape[0] // 4
    group_of = lanes_of((quarter, LANES)) // (LANES // 4)
    pieces = []
    for part in range(4):
        piece = rows[:quarter]
        for place in range(4):
            source = rows[place * quarter : (place + 1) * quarter]
            turn = (place - part) % 4
            moved = source if turn == 0 else pltpu.roll(source, turn * (LANES // 4), 1)
            piece = jnp.where(group_of == place, moved, piece)
        pieces.append(piece)
    return jnp.concatenate(pieces, 0)


def modes_kernel(s, x_ref, w_ref, field_ref, pre_ref, pack_ref, modes_ref, back):
    sums = lax.dot_general(
        field_ref[...], pre_ref[...], (((0,), (0,)), ((), ())), preferred_element_type=f32
    )
    pack_ref[:, :, 2 * LANES :] = sums.reshape(s.devices, 4, LANES).astype(bf16)
    modes_ref[...] = field_modes(s, x_ref[1, 0], x_ref[1, 1])
    groups = modes_ref.shape[0] // 8
    row = lax.broadcasted_iota(jnp.int32, (8, LANES), 0)
    lane = lanes_of((LANES, LANES))
    on_vector = [group for group in range(groups) if group * 10 // groups != (group + 1) * 10 // groups]
    kept = jnp.zeros((LANES, LANES), f32)
    for group in range(groups):
        start = group * 8
        if group in on_vector:
            for mode in range(8):
                weights = w_ref[mode, group].astype(f32)
                total = jnp.sum(weights * modes_ref[start + mode : start + mode + 1, :], 1, keepdims=True)
                kept = jnp.where(lane == on_vector.index(group) * 8 + mode, total, kept)
            continue
        every = lax.dot_general(
            modes_ref[start : start + 8, :].astype(bf16),
            w_ref[:, group].reshape(8 * LANES, LANES),
            (((1,), (1,)), ((), ())),
            preferred_element_type=f32,
        )
        total = jnp.zeros((8, LANES), f32)
        for mode in range(8):
            total = jnp.where(row == mode, every[:, mode * LANES : (mode + 1) * LANES], total)
        back[start : start + 8, :] = total
    kept = kept.T
    for at, group in enumerate(on_vector):
        back[group * 8 : group * 8 + 8, :] = kept[at * 8 : at * 8 + 8]

    rows = back[...].astype(bf16).astype(f32)
    rows = quarters(rows).reshape(s.devices, 8, LANES)
    pack_ref[:, :, :LANES] = rows[:, :4].astype(bf16)
    pack_ref[:, :, LANES : 2 * LANES] = rows[:, 4:].astype(bf16)


def outer_kernel(s, x_ref, grad_ref, pre_ref, weight_ref, after, out_hbm, part_ref, in_ref, made, sems):
    del after
    in_ref[...] = field_modes(s, x_ref[0, 0], x_ref[0, 1])
    lines, columns = made.shape[:2]
    across = 2
    size, unrolled = across * lines, 4
    groups = columns // across
    row = lax.broadcasted_iota(jnp.int32, (size, LANES), 0)

    def copy(group):
        part = pl.ds(group * across, across)
        return pltpu.make_async_copy(made.at[:, part], out_hbm.at[:, part], sems.at[group])

    @pl.loop(0, groups // unrolled)
    def _(turn):
        for at in range(unrolled):
            group = turn * unrolled + at
            start = pl.multiple_of(group * size, size)
            left = in_ref[pl.ds(start, size), :].astype(bf16)
            right = grad_ref[pl.ds(start, size), :].astype(bf16)
            zero = jnp.zeros((), bf16)
            right = jnp.concatenate([jnp.where(row == mode, right, zero) for mode in range(size)], 1)
            every = lax.dot_general(
                left, right, (((0,), (0,)), ((), ())), preferred_element_type=f32
            )
            for mode in range(size):
                part = every[:, mode * LANES : (mode + 1) * LANES].astype(bf16)
                made[mode % lines, group * across + mode // lines] = part
            copy(group).start()

    part_ref[...] = lax.dot_general(
        pre_ref[...], weight_ref[...], (((1,), (1,)), ((), ())), preferred_element_type=f32
    )

    @pl.loop(0, groups)
    def _(group):
        copy(group).wait()


def opened(got_ref):
    got = [got_ref[:, :, i * LANES : (i + 1) * LANES].astype(f32) for i in range(3)]
    return jnp.concatenate(got[:2], 1), got[2]


def back_plane_kernel(s, scale, skip_scale, got_ref, first_ref, second_ref, out_ref):
    tiles, sums = opened(got_ref)
    tiles = tiles.reshape(s.gx, s.gy, 8, LANES)
    parts = jnp.concatenate(first_axis(tiles, first_ref, s.gx, s.gy), 0)
    made = quarters(second_axis(second_ref, quarters(parts)) * scale)
    made = made.reshape(s.devices, 8, LANES)
    out_ref[:, :, :LANES] = made[:, :4].astype(bf16)
    out_ref[:, :, LANES : 2 * LANES] = made[:, 4:].astype(bf16)
    sums = jnp.sum(sums, 0, keepdims=True) * skip_scale
    out_ref[:, :, 2 * LANES :] = jnp.broadcast_to(sums, (s.devices, 4, LANES)).astype(bf16)


def close_kernel(scale, got_ref, z_ref, part_ref, out_ref, skip_ref):
    rows, sums = opened(got_ref)
    skip_ref[...] = sums
    pieces = quarters(rows.reshape(-1, LANES)).astype(bf16)
    cells = jnp.dot(z_ref[...], pieces, preferred_element_type=f32)
    out_ref[...] = (part_ref[...] + cells * scale).astype(bf16)


def one_hot(rows, columns):
    return (np.asarray(rows)[:, None] == np.asarray(columns)[None, :]).astype(np.float32)


def twice(table):
    high = table.astype(np.float32).astype(bf16)
    low = (table - high.astype(np.float64)).astype(np.float32).astype(bf16)
    return np.concatenate([high, low], 1)


def make_tables(s):
    cas_x = plain_cas(s.x * s.gx, s.x * s.gx)
    cas_y = plain_cas(s.y * s.gy, s.y * s.gy)
    cas_z = plain_cas(s.z, s.z)
    norm = math.sqrt(s.x * s.gx * s.y * s.gy)
    t = {}
    t["first"] = twice(cas_x)
    t["back_first"] = twice(cas_x.T)
    yl, py, yh, x = split_index(2 * s.gy * s.y // 2 * s.x, 2, s.gy, s.y // 2, s.x)
    at = py * s.y + yh * 2 + yl
    t["second"], factor = rounded_table(cas_y[at[:, None], at[None, :]] * one_hot(x, x))
    t["scale"] = factor / norm
    t["z_scale"] = 1.0 / math.sqrt(s.z)
    yl, py, x = split_index(4 * s.gy * s.x, 4, s.gy, s.x)
    at = py * s.y + yl
    t["back_second"], factor = rounded_table(cas_y[at[None, :], at[:, None]] * one_hot(x, x))
    t["back_scale"] = factor / norm
    x, y, z = split_index(s.cells, s.x, s.y, s.z)
    yl, c, xl = split_index(s.cells, s.y, s.z, s.x)
    t["back_z"] = one_hot(x * s.y + y, xl * s.y + yl) * cas_z[c[None, :], z[:, None]]
    return {
        key: jnp.asarray(np.asarray(value, np.float32).astype(bf16))
        if isinstance(value, np.ndarray)
        else value
        for key, value in t.items()
    }


def call(kernel, out_shape, limit, flops, moved, **more):
    return pl.pallas_call(
        kernel,
        out_shape=out_shape,
        compiler_params=pltpu.CompilerParams(vmem_limit_bytes=limit * MIB),
        cost_estimate=pl.CostEstimate(flops=flops, bytes_accessed=moved, transcendentals=0),
        **more,
    )


def in_vmem(*shape, kind=bf16):
    return pltpu.VMEM(shape, kind)


def in_hbm(*shape, kind=bf16):
    return jax.ShapeDtypeStruct(shape, kind)


def exchange(pieces):
    return lax.all_to_all(pieces, ("gx", "gy"), 0, 0)


def on_device_whole_planes(s, inputs, preact, cotangent, spectral_w, skip_w):
    t = make_tables(s)
    cells, channels, devices = s.cells, s.channels, s.devices
    rows = cells // s.z // 2 * devices
    back_rows = devices * s.x
    flat = lambda array: array.reshape(cells, channels)
    vmem = pl.BlockSpec(memory_space=pltpu.VMEM)
    hbm = pl.BlockSpec(memory_space=pltpu.HBM)
    anywhere = pl.BlockSpec(memory_space=pl.ANY)
    field = pltpu.VMEM((cells, channels), bf16)
    given = (flat(inputs), flat(preact), flat(cotangent))
    pieces, grad_pre = call(
        functools.partial(open_kernel, s),
        (in_vmem(2, 2, cells // 2, LANES), in_vmem(cells, channels)),
        16,
        1 << 40,
        MIB,
        in_specs=[hbm] * 3,
        out_specs=(vmem, vmem),
        scratch_shapes=[field, field, field, pltpu.SemaphoreType.DMA((3,))],
    )(*(pltpu.with_memory_space_constraint(a, pltpu.HBM) for a in given))
    columns = exchange(pieces.reshape(devices, -1, LANES))
    planes = call(
        functools.partial(plane_kernel, s, t["scale"] * t["z_scale"]),
        in_vmem(rows, LANES),
        16,
        1 << 31,
        MIB,
        in_specs=[vmem] * 3,
        out_specs=vmem,
    )(columns.reshape(rows, LANES), t["first"], t["second"])
    owned = exchange(planes.reshape(devices, -1, LANES))
    owned = owned.reshape(2, 2, cells // 2, LANES)
    back, grad_modes = call(
        functools.partial(modes_kernel, s),
        (
            in_vmem(devices, 4, 3 * LANES),
            in_vmem(cells, channels, kind=f32),
        ),
        24,
        cells * channels * channels * 16,
        9 * MIB,
        in_specs=[vmem] * 4,
        out_specs=(vmem, vmem),
        scratch_shapes=[pltpu.VMEM((cells, channels), f32)],
    )(
        owned,
        spectral_w.reshape(s.x, s.y * s.z, channels, channels),
        flat(inputs),
        grad_pre,
    )
    got = exchange(back)
    back_planes = call(
        functools.partial(
            back_plane_kernel, s, t["back_scale"], 1.0 / math.sqrt(cells * devices)
        ),
        in_hbm(devices, 4, 3 * LANES),
        16,
        back_rows * back_rows * LANES * 8,
        MIB,
        in_specs=[vmem] * 3,
        out_specs=vmem,
    )(got, t["back_first"], t["back_second"])
    split_modes = (s.x, s.y * s.z, channels, channels)
    split_modes = (s.x, s.y * s.z, channels, channels)
    grad_spectral, skip_part = call(
        functools.partial(outer_kernel, s),
        (in_hbm(*split_modes), in_vmem(cells, channels, kind=f32)),
        24,
        cells * channels * channels * 2,
        9 * MIB,
        in_specs=[vmem] * 4 + [anywhere],
        out_specs=(hbm, vmem),
        scratch_shapes=[
            pltpu.VMEM((cells, channels), f32),
            pltpu.VMEM(split_modes, bf16),
            pltpu.SemaphoreType.DMA((s.y * s.z // 2,)),
        ],
    )(owned, grad_modes, grad_pre, skip_w, back_planes)
    got = exchange(back_planes)
    grad_inputs, grad_skip = call(
        functools.partial(close_kernel, t["z_scale"]),
        (in_hbm(cells, channels), in_hbm(devices, 4, channels, kind=f32)),
        16,
        cells * cells * LANES * 4,
        MIB,
        in_specs=[vmem] * 3,
        out_specs=(vmem, vmem),
    )(got, t["back_z"], skip_part)
    return (
        grad_inputs.reshape(inputs.shape),
        grad_spectral.reshape(spectral_w.shape),
        grad_skip.reshape(channels, channels),
    )


def on_device(inputs, preact, cotangent, spectral_w, skip_w):
    sizes = Sizes(inputs, spectral_w, lax.axis_size("gx"), lax.axis_size("gy"))
    if sizes.fits(inputs, spectral_w):
        return on_device_whole_planes(sizes, inputs, preact, cotangent, spectral_w, skip_w)
    return on_device_any(inputs, preact, cotangent, spectral_w, skip_w)


def on_device_any(inputs, preact, cotangent, spectral_w, skip_w):
    cells_x, cells_y, cells_z, channels = inputs.shape
    length_x = cells_x * lax.axis_size("gx")
    length_y = cells_y * lax.axis_size("gy")
    local_modes_x, local_modes_y, modes_z = (
        spectral_w.shape[0],
        spectral_w.shape[1],
        spectral_w.shape[2],
    )
    modes_x = local_modes_x * lax.axis_size("gx")
    modes_y = local_modes_y * lax.axis_size("gy")
    table_z = cas_table(modes_z, cells_z, 0, cells_z)
    table_x = cas_table(modes_x, length_x, lax.axis_index("gx") * cells_x, cells_x)
    table_y = cas_table(modes_y, length_y, lax.axis_index("gy") * cells_y, cells_y)
    preact_wide = preact.astype(jnp.float32)
    gelu_slope = 0.5 * (
        1.0 + lax.erf(preact_wide * (1.0 / math.sqrt(2.0)))
    ) + preact_wide * jnp.exp(-0.5 * preact_wide * preact_wide) * (1.0 / math.sqrt(2.0 * math.pi))
    grad_pre = (cotangent.astype(jnp.float32) * gelu_slope).astype(jnp.bfloat16)
    fields = jnp.stack([inputs, grad_pre]).astype(jnp.float32)
    z_modes = jnp.einsum("ck,fijkh->fijch", table_z, fields, precision=highest)
    table_rows = table_y
    part_y = lax.psum_scatter(
        jnp.einsum("bj,fijch->bfich", table_rows, z_modes, precision=highest),
        "gy",
        scatter_dimension=0,
        tiled=True,
    )
    table_rows = table_x
    owned_modes = lax.psum_scatter(
        jnp.einsum("ai,bfich->abfch", table_rows, part_y, precision=highest),
        "gx",
        scatter_dimension=0,
        tiled=True,
    )
    input_modes = owned_modes[:, :, 0]
    grad_modes = owned_modes[:, :, 1]
    grad_spectral = jnp.einsum(
        "abcp,abcq->abcpq", input_modes, grad_modes, precision=highest
    ).astype(jnp.bfloat16)
    back_modes = jnp.einsum(
        "abcq,abcpq->abcp", grad_modes, spectral_w.astype(jnp.float32), precision=highest
    ).astype(jnp.bfloat16)
    table_rows = table_x
    over_first = jnp.einsum(
        "ai,abch->ibch",
        table_rows,
        lax.all_gather(back_modes, "gx", axis=0, tiled=True).astype(jnp.float32),
        precision=highest,
    )
    table_rows = table_y
    cell_modes = jnp.einsum(
        "bj,ibch->ijch",
        table_rows,
        lax.all_gather(over_first, "gy", axis=1, tiled=True),
        precision=highest,
    )
    spectral_cells = jnp.einsum("ck,ijch->ijkh", table_z, cell_modes, precision=highest)
    flat_grad = grad_pre.reshape(-1, channels)
    skip_part = lax.dot_general(
        flat_grad, skip_w, (((1,), (1,)), ((), ())), preferred_element_type=jnp.float32
    )
    grad_inputs = (skip_part.reshape(cells_x, cells_y, cells_z, channels) + spectral_cells).astype(
        jnp.bfloat16
    )
    local_sum = lax.dot_general(
        inputs.reshape(-1, channels),
        flat_grad,
        (((0,), (0,)), ((), ())),
        preferred_element_type=jnp.float32,
    )
    grad_skip = lax.psum(local_sum, ("gx", "gy")) / math.sqrt(length_x * length_y * cells_z)
    return (grad_inputs, grad_spectral, grad_skip)


def solution(mesh):
    in_specs = (
        P("gx", "gy", None, None),
        P("gx", "gy", None, None),
        P("gx", "gy", None, None),
        P("gx", "gy", None, None, None),
        P(),
    )
    out_specs = (P("gx", "gy", None, None), P("gx", "gy", None, None, None), P())
    return jax.shard_map(
        on_device, mesh=mesh, in_specs=in_specs, out_specs=out_specs, check_vma=False
    )
```

```python
import functools
import math

import jax
import jax.numpy as jnp
import numpy as np
from jax import lax
from jax.experimental import pallas as pl
from jax.experimental.pallas import tpu as pltpu
from jax.sharding import PartitionSpec as P

highest = lax.Precision.HIGHEST
f32 = jnp.float32
bf16 = jnp.bfloat16
LANES = 128
MIB = 1 << 20


def cas_table(modes, length, offset, cells):
    index = jnp.arange(modes, dtype=jnp.int32)
    freq = jnp.where(index < modes // 2, index, length - modes + index)
    where_cells = offset + jnp.arange(cells, dtype=jnp.int32)
    phase = freq[:, None] * where_cells[None, :] % length
    angle = phase.astype(jnp.float32) * (2.0 * math.pi / length)
    return (jnp.cos(angle) + jnp.sin(angle)) / math.sqrt(length)


def gelu_slope_of(preact_wide):
    return 0.5 * (
        1.0 + lax.erf(preact_wide * (1.0 / math.sqrt(2.0)))
    ) + preact_wide * jnp.exp(-0.5 * preact_wide * preact_wide) * (1.0 / math.sqrt(2.0 * math.pi))


def plain_cas(modes, length):
    index = np.arange(modes)
    freq = np.where(index < modes // 2, index, length - modes + index)
    angle = 2.0 * np.pi * ((freq[:, None] * np.arange(length)[None, :]) % length) / length
    return np.cos(angle) + np.sin(angle)


def rounded_table(table):
    values, counts = np.unique(np.round(np.abs(table), 12), return_counts=True)
    best = None
    for scale in np.linspace(1.0, 2.0, 512, endpoint=False):
        kept = (values * scale).astype(np.float32).astype(bf16).astype(np.float64) / scale
        error = np.sum(counts * (kept - values) ** 2)
        if best is None or error < best[0]:
            best = (error, scale)
    return (table * best[1]).astype(np.float32).astype(bf16), 1.0 / best[1]


def split_index(size, *parts):
    return np.unravel_index(np.arange(size), parts)


class Sizes:
    def __init__(self, inputs, spectral_w, gx, gy):
        self.gx, self.gy = gx, gy
        self.devices = gx * gy
        self.x, self.y, self.z, self.channels = inputs.shape
        self.cells = self.x * self.y * self.z
        self.width = 2 * self.z * self.channels // self.devices
        self.back_width = self.z * self.channels // self.devices

    def fits(self, inputs, spectral_w):
        if inputs.shape[:3] != spectral_w.shape[:3] or self.channels != LANES:
            return False
        if self.back_width * 4 != LANES or self.y % 4:
            return False
        rows = self.x * self.y // 2
        return rows == 16 and self.devices * 4 == LANES and self.x * self.y // 4 == 8 and self.z == 8


def lanes_of(shape):
    return lax.broadcasted_iota(jnp.int32, shape, len(shape) - 1)


def load(*pairs):
    copies = [pltpu.make_async_copy(source, target, sem) for source, target, sem in pairs]
    for copy in copies:
        copy.start()
    return copies


def open_kernel(s, in_hbm, pre_hbm, cot_hbm, pack_ref, grad_ref, in_ref, pre_ref, cot_ref, sems):
    copies = load(
        (in_hbm, in_ref, sems.at[0]),
        (pre_hbm, pre_ref, sems.at[1]),
        (cot_hbm, cot_ref, sems.at[2]),
    )
    cells = s.cells
    place = lax.broadcasted_iota(jnp.int32, (cells, 1), 0)
    half_y, half = s.y // 2, cells // 2
    yl, rest = place // half, place % half
    mode, rest = rest // (s.x * half_y), rest % (s.x * half_y)
    yh, x = rest // s.x, rest % s.x
    source = lax.broadcasted_iota(jnp.int32, (1, cells), 1)
    phase = mode * (source % s.z) % s.z
    table = jnp.zeros((cells, cells), f32)
    for value in range(s.z):
        angle = 2.0 * math.pi * value / s.z
        table = jnp.where(phase == value, math.cos(angle) + math.sin(angle), table)
    table = jnp.where(x * s.y + yh * 2 + yl == source // s.z, table, 0.0).astype(bf16)
    for copy in copies:
        copy.wait()
    grad = (cot_ref[...].astype(f32) * gelu_slope_of(pre_ref[...].astype(f32))).astype(bf16)
    grad_ref[...] = grad
    rows = jnp.dot(
        table, jnp.concatenate([in_ref[...], grad], 1), preferred_element_type=f32
    )
    width = LANES // 2
    half = rows.shape[0] // 2
    low = lanes_of((half, LANES)) < width
    for field in range(2):
        even = rows[:half, field * LANES : (field + 1) * LANES]
        odd = rows[half:, field * LANES : (field + 1) * LANES]
        pack_ref[field, 0] = jnp.where(low, even, pltpu.roll(odd, width, 1)).astype(bf16)
        pack_ref[field, 1] = jnp.where(low, pltpu.roll(even, width, 1), odd).astype(bf16)


def first_axis(tiles, table_ref, along, across):
    lines = [tiles[:, j].reshape(along * 8, LANES) for j in range(across)]
    lines = jnp.concatenate(lines, 1).astype(bf16)
    made = jnp.dot(
        table_ref[...], jnp.concatenate([lines, lines], 0), preferred_element_type=f32
    )
    return [
        jnp.concatenate(
            [made[i * 8 : i * 8 + 8, j * LANES : (j + 1) * LANES] for j in range(across)], 0
        )
        for i in range(along)
    ]


def halves(first, second):
    width = LANES // 2
    low = lanes_of(first.shape) < width
    return (
        jnp.where(low, first, pltpu.roll(second, width, 1)),
        jnp.where(low, pltpu.roll(first, width, 1), second),
    )


def second_axis(table_ref, value):
    table = table_ref[...]
    return jnp.dot(
        jnp.concatenate([table, table], 1),
        jnp.concatenate(split_twice(value), 0),
        preferred_element_type=f32,
    )


def plane_kernel(s, scale, x_ref, first_ref, second_ref, out_ref):
    across = s.gy * s.y // 2
    tiles = x_ref[...].astype(f32).reshape(s.gx, across, 8, LANES)
    parts = first_axis(tiles, first_ref, s.gx, across)
    pairs = [jnp.concatenate(halves(*parts[i : i + 2]), 0) for i in range(0, s.gx, 2)]
    made = second_axis(second_ref, jnp.concatenate(pairs, 1)) * scale
    rows = across * 8
    for pair in range(s.gx // 2):
        here = made[:, pair * LANES : (pair + 1) * LANES]
        for i, value in enumerate(halves(here[:rows], here[rows:])):
            start = (pair * 2 + i) * rows
            out_ref[start : start + rows, :] = value.astype(bf16)


def field_modes(s, first, second):
    width = LANES // 2
    first, second = first.astype(f32), second.astype(f32)
    low = lanes_of(first.shape) < width
    even = jnp.where(low, first, pltpu.roll(second, width, 1))
    odd = jnp.where(low, pltpu.roll(first, width, 1), second)
    even, odd = (value.reshape(s.z, s.y // 2, s.x, LANES) for value in (even, odd))
    lines = [value[:, half].reshape(s.z * s.x, LANES) for half in range(s.y // 2) for value in (even, odd)]
    return jnp.concatenate(lines, 0)


def split_twice(value):
    high = value.astype(bf16)
    return high, (value - high.astype(f32)).astype(bf16)


def quarters(rows):
    quarter = rows.shape[0] // 4
    group_of = lanes_of((quarter, LANES)) // (LANES // 4)
    pieces = []
    for part in range(4):
        piece = rows[:quarter]
        for place in range(4):
            source = rows[place * quarter : (place + 1) * quarter]
            turn = (place - part) % 4
            moved = source if turn == 0 else pltpu.roll(source, turn * (LANES // 4), 1)
            piece = jnp.where(group_of == place, moved, piece)
        pieces.append(piece)
    return jnp.concatenate(pieces, 0)


def modes_kernel(s, x_ref, w_ref, field_ref, pre_ref, pack_ref, modes_ref, back):
    sums = lax.dot_general(
        field_ref[...], pre_ref[...], (((0,), (0,)), ((), ())), preferred_element_type=f32
    )
    pack_ref[:, :, 2 * LANES :] = sums.reshape(s.devices, 4, LANES).astype(bf16)
    modes_ref[...] = field_modes(s, x_ref[1, 0], x_ref[1, 1])
    groups = modes_ref.shape[0] // 8
    row = lax.broadcasted_iota(jnp.int32, (8, LANES), 0)
    on_vector = [group for group in range(groups) if group * 10 // groups != (group + 1) * 10 // groups]
    for group in range(groups):
        start = group * 8
        if group in on_vector:
            for mode in range(8):
                weights = w_ref[mode, group].astype(f32)
                product = weights * modes_ref[start + mode : start + mode + 1, :]
                back[start + mode : start + mode + 1, :] = jnp.sum(product.T, 0, keepdims=True)
            continue
        every = lax.dot_general(
            modes_ref[start : start + 8, :].astype(bf16),
            w_ref[:, group].reshape(8 * LANES, LANES),
            (((1,), (1,)), ((), ())),
            preferred_element_type=f32,
        )
        total = jnp.zeros((8, LANES), f32)
        for mode in range(8):
            total = jnp.where(row == mode, every[:, mode * LANES : (mode + 1) * LANES], total)
        back[start : start + 8, :] = total
    rows = back[...].astype(bf16).astype(f32)
    rows = quarters(rows).reshape(s.devices, 8, LANES)
    pack_ref[:, :, :LANES] = rows[:, :4].astype(bf16)
    pack_ref[:, :, LANES : 2 * LANES] = rows[:, 4:].astype(bf16)


def outer_kernel(s, x_ref, grad_ref, pre_ref, weight_ref, after, out_hbm, part_ref, in_ref, made, sems):
    del after
    in_ref[...] = field_modes(s, x_ref[0, 0], x_ref[0, 1])
    lines, columns = made.shape[:2]
    across = 2
    size, unrolled = across * lines, 4
    groups = columns // across
    row = lax.broadcasted_iota(jnp.int32, (size, LANES), 0)

    def copy(group):
        part = pl.ds(group * across, across)
        return pltpu.make_async_copy(made.at[:, part], out_hbm.at[:, part], sems.at[group])

    @pl.loop(0, groups // unrolled)
    def _(turn):
        for at in range(unrolled):
            group = turn * unrolled + at
            start = pl.multiple_of(group * size, size)
            left = in_ref[pl.ds(start, size), :].astype(bf16)
            right = grad_ref[pl.ds(start, size), :].astype(bf16)
            zero = jnp.zeros((), bf16)
            right = jnp.concatenate([jnp.where(row == mode, right, zero) for mode in range(size)], 1)
            every = lax.dot_general(
                left, right, (((0,), (0,)), ((), ())), preferred_element_type=f32
            )
            for mode in range(size):
                part = every[:, mode * LANES : (mode + 1) * LANES].astype(bf16)
                made[mode % lines, group * across + mode // lines] = part
            copy(group).start()

    part_ref[...] = lax.dot_general(
        pre_ref[...], weight_ref[...], (((1,), (1,)), ((), ())), preferred_element_type=f32
    )

    @pl.loop(0, groups)
    def _(group):
        copy(group).wait()


def opened(got_ref):
    got = [got_ref[:, :, i * LANES : (i + 1) * LANES].astype(f32) for i in range(3)]
    return jnp.concatenate(got[:2], 1), got[2]


def back_plane_kernel(s, scale, skip_scale, got_ref, first_ref, second_ref, out_ref):
    tiles, sums = opened(got_ref)
    tiles = tiles.reshape(s.gx, s.gy, 8, LANES)
    parts = jnp.concatenate(first_axis(tiles, first_ref, s.gx, s.gy), 0)
    made = quarters(second_axis(second_ref, quarters(parts)) * scale)
    made = made.reshape(s.devices, 8, LANES)
    out_ref[:, :, :LANES] = made[:, :4].astype(bf16)
    out_ref[:, :, LANES : 2 * LANES] = made[:, 4:].astype(bf16)
    sums = jnp.sum(sums, 0, keepdims=True) * skip_scale
    out_ref[:, :, 2 * LANES :] = jnp.broadcast_to(sums, (s.devices, 4, LANES)).astype(bf16)


def close_kernel(scale, got_ref, z_ref, part_ref, out_ref, skip_ref):
    rows, sums = opened(got_ref)
    skip_ref[...] = sums
    pieces = quarters(rows.reshape(-1, LANES)).astype(bf16)
    cells = jnp.dot(z_ref[...], pieces, preferred_element_type=f32)
    out_ref[...] = (part_ref[...] + cells * scale).astype(bf16)


def one_hot(rows, columns):
    return (np.asarray(rows)[:, None] == np.asarray(columns)[None, :]).astype(np.float32)


def twice(table):
    high = table.astype(np.float32).astype(bf16)
    low = (table - high.astype(np.float64)).astype(np.float32).astype(bf16)
    return np.concatenate([high, low], 1)


def make_tables(s):
    cas_x = plain_cas(s.x * s.gx, s.x * s.gx)
    cas_y = plain_cas(s.y * s.gy, s.y * s.gy)
    cas_z = plain_cas(s.z, s.z)
    norm = math.sqrt(s.x * s.gx * s.y * s.gy)
    t = {}
    t["first"] = twice(cas_x)
    t["back_first"] = twice(cas_x.T)
    yl, py, yh, x = split_index(2 * s.gy * s.y // 2 * s.x, 2, s.gy, s.y // 2, s.x)
    at = py * s.y + yh * 2 + yl
    t["second"], factor = rounded_table(cas_y[at[:, None], at[None, :]] * one_hot(x, x))
    t["scale"] = factor / norm
    t["z_scale"] = 1.0 / math.sqrt(s.z)
    yl, py, x = split_index(4 * s.gy * s.x, 4, s.gy, s.x)
    at = py * s.y + yl
    t["back_second"], factor = rounded_table(cas_y[at[None, :], at[:, None]] * one_hot(x, x))
    t["back_scale"] = factor / norm
    x, y, z = split_index(s.cells, s.x, s.y, s.z)
    yl, c, xl = split_index(s.cells, s.y, s.z, s.x)
    t["back_z"] = one_hot(x * s.y + y, xl * s.y + yl) * cas_z[c[None, :], z[:, None]]
    return {
        key: jnp.asarray(np.asarray(value, np.float32).astype(bf16))
        if isinstance(value, np.ndarray)
        else value
        for key, value in t.items()
    }


def call(kernel, out_shape, limit, flops, moved, **more):
    return pl.pallas_call(
        kernel,
        out_shape=out_shape,
        compiler_params=pltpu.CompilerParams(vmem_limit_bytes=limit * MIB),
        cost_estimate=pl.CostEstimate(flops=flops, bytes_accessed=moved, transcendentals=0),
        **more,
    )


def in_vmem(*shape, kind=bf16):
    return pltpu.VMEM(shape, kind)


def in_hbm(*shape, kind=bf16):
    return jax.ShapeDtypeStruct(shape, kind)


def exchange(pieces):
    return lax.all_to_all(pieces, ("gx", "gy"), 0, 0)


def on_device_whole_planes(s, inputs, preact, cotangent, spectral_w, skip_w):
    t = make_tables(s)
    cells, channels, devices = s.cells, s.channels, s.devices
    rows = cells // s.z // 2 * devices
    back_rows = devices * s.x
    flat = lambda array: array.reshape(cells, channels)
    vmem = pl.BlockSpec(memory_space=pltpu.VMEM)
    hbm = pl.BlockSpec(memory_space=pltpu.HBM)
    anywhere = pl.BlockSpec(memory_space=pl.ANY)
    field = pltpu.VMEM((cells, channels), bf16)
    given = (flat(inputs), flat(preact), flat(cotangent))
    pieces, grad_pre = call(
        functools.partial(open_kernel, s),
        (in_vmem(2, 2, cells // 2, LANES), in_vmem(cells, channels)),
        16,
        1 << 40,
        MIB,
        in_specs=[hbm] * 3,
        out_specs=(vmem, vmem),
        scratch_shapes=[field, field, field, pltpu.SemaphoreType.DMA((3,))],
    )(*(pltpu.with_memory_space_constraint(a, pltpu.HBM) for a in given))
    columns = exchange(pieces.reshape(devices, -1, LANES))
    planes = call(
        functools.partial(plane_kernel, s, t["scale"] * t["z_scale"]),
        in_vmem(rows, LANES),
        16,
        1 << 31,
        MIB,
        in_specs=[vmem] * 3,
        out_specs=vmem,
    )(columns.reshape(rows, LANES), t["first"], t["second"])
    owned = exchange(planes.reshape(devices, -1, LANES))
    owned = owned.reshape(2, 2, cells // 2, LANES)
    back, grad_modes = call(
        functools.partial(modes_kernel, s),
        (
            in_vmem(devices, 4, 3 * LANES),
            in_vmem(cells, channels, kind=f32),
        ),
        24,
        cells * channels * channels * 16,
        9 * MIB,
        in_specs=[vmem] * 4,
        out_specs=(vmem, vmem),
        scratch_shapes=[pltpu.VMEM((cells, channels), f32)],
    )(
        owned,
        spectral_w.reshape(s.x, s.y * s.z, channels, channels),
        flat(inputs),
        grad_pre,
    )
    got = exchange(back)
    back_planes = call(
        functools.partial(
            back_plane_kernel, s, t["back_scale"], 1.0 / math.sqrt(cells * devices)
        ),
        in_hbm(devices, 4, 3 * LANES),
        16,
        back_rows * back_rows * LANES * 8,
        MIB,
        in_specs=[vmem] * 3,
        out_specs=vmem,
    )(got, t["back_first"], t["back_second"])
    split_modes = (s.x, s.y * s.z, channels, channels)
    split_modes = (s.x, s.y * s.z, channels, channels)
    grad_spectral, skip_part = call(
        functools.partial(outer_kernel, s),
        (in_hbm(*split_modes), in_vmem(cells, channels, kind=f32)),
        24,
        cells * channels * channels * 2,
        9 * MIB,
        in_specs=[vmem] * 4 + [anywhere],
        out_specs=(hbm, vmem),
        scratch_shapes=[
            pltpu.VMEM((cells, channels), f32),
            pltpu.VMEM(split_modes, bf16),
            pltpu.SemaphoreType.DMA((s.y * s.z // 2,)),
        ],
    )(owned, grad_modes, grad_pre, skip_w, back_planes)
    got = exchange(back_planes)
    grad_inputs, grad_skip = call(
        functools.partial(close_kernel, t["z_scale"]),
        (in_hbm(cells, channels), in_hbm(devices, 4, channels, kind=f32)),
        16,
        cells * cells * LANES * 4,
        MIB,
        in_specs=[vmem] * 3,
        out_specs=(vmem, vmem),
    )(got, t["back_z"], skip_part)
    return (
        grad_inputs.reshape(inputs.shape),
        grad_spectral.reshape(spectral_w.shape),
        grad_skip.reshape(channels, channels),
    )


def on_device(inputs, preact, cotangent, spectral_w, skip_w):
    sizes = Sizes(inputs, spectral_w, lax.axis_size("gx"), lax.axis_size("gy"))
    if sizes.fits(inputs, spectral_w):
        return on_device_whole_planes(sizes, inputs, preact, cotangent, spectral_w, skip_w)
    return on_device_any(inputs, preact, cotangent, spectral_w, skip_w)


def on_device_any(inputs, preact, cotangent, spectral_w, skip_w):
    cells_x, cells_y, cells_z, channels = inputs.shape
    length_x = cells_x * lax.axis_size("gx")
    length_y = cells_y * lax.axis_size("gy")
    local_modes_x, local_modes_y, modes_z = (
        spectral_w.shape[0],
        spectral_w.shape[1],
        spectral_w.shape[2],
    )
    modes_x = local_modes_x * lax.axis_size("gx")
    modes_y = local_modes_y * lax.axis_size("gy")
    table_z = cas_table(modes_z, cells_z, 0, cells_z)
    table_x = cas_table(modes_x, length_x, lax.axis_index("gx") * cells_x, cells_x)
    table_y = cas_table(modes_y, length_y, lax.axis_index("gy") * cells_y, cells_y)
    preact_wide = preact.astype(jnp.float32)
    gelu_slope = 0.5 * (
        1.0 + lax.erf(preact_wide * (1.0 / math.sqrt(2.0)))
    ) + preact_wide * jnp.exp(-0.5 * preact_wide * preact_wide) * (1.0 / math.sqrt(2.0 * math.pi))
    grad_pre = (cotangent.astype(jnp.float32) * gelu_slope).astype(jnp.bfloat16)
    fields = jnp.stack([inputs, grad_pre]).astype(jnp.float32)
    z_modes = jnp.einsum("ck,fijkh->fijch", table_z, fields, precision=highest)
    table_rows = table_y
    part_y = lax.psum_scatter(
        jnp.einsum("bj,fijch->bfich", table_rows, z_modes, precision=highest),
        "gy",
        scatter_dimension=0,
        tiled=True,
    )
    table_rows = table_x
    owned_modes = lax.psum_scatter(
        jnp.einsum("ai,bfich->abfch", table_rows, part_y, precision=highest),
        "gx",
        scatter_dimension=0,
        tiled=True,
    )
    input_modes = owned_modes[:, :, 0]
    grad_modes = owned_modes[:, :, 1]
    grad_spectral = jnp.einsum(
        "abcp,abcq->abcpq", input_modes, grad_modes, precision=highest
    ).astype(jnp.bfloat16)
    back_modes = jnp.einsum(
        "abcq,abcpq->abcp", grad_modes, spectral_w.astype(jnp.float32), precision=highest
    ).astype(jnp.bfloat16)
    table_rows = table_x
    over_first = jnp.einsum(
        "ai,abch->ibch",
        table_rows,
        lax.all_gather(back_modes, "gx", axis=0, tiled=True).astype(jnp.float32),
        precision=highest,
    )
    table_rows = table_y
    cell_modes = jnp.einsum(
        "bj,ibch->ijch",
        table_rows,
        lax.all_gather(over_first, "gy", axis=1, tiled=True),
        precision=highest,
    )
    spectral_cells = jnp.einsum("ck,ijch->ijkh", table_z, cell_modes, precision=highest)
    flat_grad = grad_pre.reshape(-1, channels)
    skip_part = lax.dot_general(
        flat_grad, skip_w, (((1,), (1,)), ((), ())), preferred_element_type=jnp.float32
    )
    grad_inputs = (skip_part.reshape(cells_x, cells_y, cells_z, channels) + spectral_cells).astype(
        jnp.bfloat16
    )
    local_sum = lax.dot_general(
        inputs.reshape(-1, channels),
        flat_grad,
        (((0,), (0,)), ((), ())),
        preferred_element_type=jnp.float32,
    )
    grad_skip = lax.psum(local_sum, ("gx", "gy")) / math.sqrt(length_x * length_y * cells_z)
    return (grad_inputs, grad_spectral, grad_skip)


def solution(mesh):
    in_specs = (
        P("gx", "gy", None, None),
        P("gx", "gy", None, None),
        P("gx", "gy", None, None),
        P("gx", "gy", None, None, None),
        P(),
    )
    out_specs = (P("gx", "gy", None, None), P("gx", "gy", None, None, None), P())
    return jax.shard_map(
        on_device, mesh=mesh, in_specs=in_specs, out_specs=out_specs, check_vma=False
    )
```
